512 devices in a mesh: section: 8 (over x, core), fsdp: 16 (over z_lo, y), tp: 4 (over z_hi).
Axes of the slice: x: 4, y: 8, z: 8 (z_hi: 4, z_lo: 2; z = z_hi * 2 + z_lo), core: 2. Of those that a mesh axis runs over, the one named last changes fastest.
Arguments:
- queries: bfloat16 [8, 2048, 4096], P('section', 'fsdp', 'tp'), may hold values from -160 to 160
- key_rows: bfloat16 [8, 2048, 512], P('section', 'fsdp', 'tp'), may hold values from -8 to 8
- values: bfloat16 [8, 2048, 512], P('section', 'fsdp', 'tp'), may hold values from -6 to 6
- segments: int32 [8, 2048], P('section', 'fsdp'), may hold values from 0 to 15, never falling along the last dimension, each value on 1 to 1152 neighbouring positions
- held_queries: bfloat16 [8, 2048, 4096], P('section', ('fsdp', 'tp')), may hold values from -160 to 160
- held_keys: bfloat16 [8, 2048, 512], P('section', ('fsdp', 'tp')), may hold values from -8 to 8
- held_values: bfloat16 [8, 2048, 512], P('section', ('fsdp', 'tp')), may hold values from -6 to 6
- held_segments: int32 [8, 2048], P('section', 'fsdp'), may hold values from 0 to 15, never falling along the last dimension, each value on 1 to 1152 neighbouring positions
- out_grad: bfloat16 [8, 2048, 4096], P('section', 'fsdp', 'tp'), may hold values from -6 to 6
Outputs:
- attn_out: bfloat16 [8, 2048, 4096], P('section', 'fsdp', 'tp')
- query_grad: bfloat16 [8, 2048, 4096], P('section', 'fsdp', 'tp')
- key_grad: bfloat16 [8, 2048, 512], P('section', 'fsdp', 'tp')
- value_grad: bfloat16 [8, 2048, 512], P('section', 'fsdp', 'tp')
The draws below stay inside these ranges and needn't reach their ends.
All inputs are finite; a program needn't handle non-finite values.
Results may differ from the reference program's by a relative error of at most 0.014.
Values may be sent and summed in bfloat16 or wider, within the bound.
No kernel may reach another device: no remote copies, remote signals or barrier semaphores. Data moves between devices by JAX's collectives and lax.ppermute only.
A program may use at most 64 MiB of HBM per device.

```python
import math
import jax
import jax.numpy as jnp
import numpy as np
from jax import lax

TOK_DEV = 128
HEADS = 32
KV_HEADS = 4
HEAD_DIM = 128
SECTIONS = 8
SEQ = 2048
N_FSDP = 16


def paired_draw(key, salt):
    base_key = jax.random.fold_in(key, salt)
    key_field = jax.random.normal(jax.random.fold_in(base_key, 1), (SECTIONS, SEQ, KV_HEADS, HEAD_DIM), jnp.float32)
    query_field = jax.random.normal(jax.random.fold_in(base_key, 2), (SECTIONS, SEQ, KV_HEADS, HEADS // KV_HEADS, HEAD_DIM), jnp.float32)
    return (query_field, key_field)


def draw_queries(key, part):
    query_field, key_field = paired_draw(key, 5)
    return query_field.reshape(SECTIONS, SEQ, HEADS * HEAD_DIM).astype(jnp.bfloat16)


def draw_key_rows(key, part):
    query_field, key_field = paired_draw(key, 5)
    return key_field.reshape(SECTIONS, SEQ, KV_HEADS * HEAD_DIM).astype(jnp.bfloat16)


def draw_held_queries(key, part):
    query_field, key_field = paired_draw(key, 7)
    return query_field.reshape(SECTIONS, SEQ, HEADS * HEAD_DIM).astype(jnp.bfloat16)


def draw_held_keys(key, part):
    query_field, key_field = paired_draw(key, 7)
    return key_field.reshape(SECTIONS, SEQ, KV_HEADS * HEAD_DIM).astype(jnp.bfloat16)


def block_scale(stream_key, dims, cuts, smallest, high):
    factor_of, own = 1.0, jax.random.fold_in(stream_key, 6)
    for dim, shards_of in cuts:
        draws = jnp.exp(jax.random.uniform(jax.random.fold_in(own, dim), (shards_of,), jnp.float32, smallest / len(cuts), high / len(cuts)))
        factor_of = factor_of * jnp.repeat(draws, dims[dim] // shards_of).reshape([-1 if axis == dim else 1 for axis in range(len(dims))])
    return factor_of


def split_up(number_of, total, most, skew):
    portions = [(1 << 20) // math.isqrt(standing ** skew) + 1 for standing in range(2, number_of + 1)]
    surplus, given = total - most - (number_of - 1), [1] * (number_of - 1)
    while surplus > 0:
        movable = [i for i in range(number_of - 1) if given[i] < most]
        whole, left = sum([portions[i] for i in movable]), surplus
        for i in movable:
            extra = min(most - given[i], max(1, left * portions[i] // whole), surplus)
            given[i] = given[i] + extra
            surplus = surplus - extra
    return np.array([most] + given)


def ragged_sizes(stream_key, amount, total, most, slope):
    if amount == 2:
        one = jax.random.randint(stream_key, (), max(1, total - most), min(most, total - 1) + 1)
        return jnp.stack([one, total - one])
    lengths = jnp.asarray(split_up(amount, total, most, slope), jnp.int32)
    twos = (amount - 1) // 2
    source_of, receiver = lengths[1:1 + 2 * twos:2], lengths[2:2 + 2 * twos:2]
    margin = jnp.minimum(source_of - 1, most - receiver)
    moved = jax.random.randint(jax.random.fold_in(stream_key, 1), (twos,), 0, 1 << 20) % (margin + 1)
    lengths = lengths.at[1:1 + 2 * twos:2].set(source_of - moved).at[2:2 + 2 * twos:2].set(receiver + moved)
    return lengths[jax.random.permutation(jax.random.fold_in(stream_key, 2), amount)]


def centred(own_key, shape, width, reach, cuts=(), held_as=jnp.bfloat16):
    level = block_scale(own_key, shape, cuts, -0.22, 0.18) if cuts else 1.0
    entries = jax.random.normal(own_key, shape, jnp.float32) * width * level
    return jnp.minimum(jnp.maximum(entries, -reach), reach).astype(held_as)


def setup_inputs(seed: int = 0) -> dict:
    key_of = jax.random.split(jax.random.key(seed), 10)
    queries = draw_queries(jax.random.fold_in(key_of[9], 71), 0)
    key_rows = draw_key_rows(jax.random.fold_in(key_of[9], 71), 0)
    values = centred(key_of[2], (SECTIONS, SEQ, KV_HEADS * HEAD_DIM), 1.0, 6.0, ((0, 8), (1, 16), (2, 4)))
    segments = jax.vmap(lambda own: jnp.searchsorted(jnp.cumsum(ragged_sizes(own, N_FSDP, SEQ, SEQ // 2 + TOK_DEV, 2)), jnp.arange(SEQ), side="right"))(jax.random.split(key_of[3], SECTIONS)).reshape((SECTIONS, SEQ)).astype(jnp.int32)
    held_queries = draw_held_queries(jax.random.fold_in(key_of[9], 71), 0)
    held_keys = draw_held_keys(jax.random.fold_in(key_of[9], 71), 0)
    held_values = centred(key_of[6], (SECTIONS, SEQ, KV_HEADS * HEAD_DIM), 1.0, 6.0, ((0, 8), (1, 64)))
    held_segments = jax.vmap(lambda own: jnp.searchsorted(jnp.cumsum(ragged_sizes(own, N_FSDP, SEQ, SEQ // 2 + TOK_DEV, 2)), jnp.arange(SEQ), side="right"))(jax.random.split(key_of[7], SECTIONS)).reshape((SECTIONS, SEQ)).astype(jnp.int32)
    out_grad = centred(key_of[8], (SECTIONS, SEQ, HEADS * HEAD_DIM), 1.0, 6.0, ((0, 8), (1, 16), (2, 4)))
    return dict(queries=queries, key_rows=key_rows, values=values, segments=segments, held_queries=held_queries, held_keys=held_keys, held_values=held_values, held_segments=held_segments, out_grad=out_grad)


NEG = -1e+30

def visible_pairs(seg_row):
    position = jnp.arange(seg_row.shape[0], dtype=jnp.int32)
    return (position[None, :] <= position[:, None]) & (seg_row[None, :] == seg_row[:, None])

def lowered(array):
    return lax.optimization_barrier(array.astype(jnp.bfloat16)).astype(jnp.float32)

def group_scores(query_group, key_group):
    scores = jnp.einsum('ird,jd->irj', query_group.astype(jnp.float32), key_group.astype(jnp.float32), precision=lax.Precision.HIGHEST)
    return scores * (1.0 / math.sqrt(HEAD_DIM))

def group_forward(query_group, key_group, value_group, visible):
    visible_wide = visible[:, None, :]
    scores = jnp.where(visible_wide, group_scores(query_group, key_group), NEG)
    row_max = lax.optimization_barrier(jnp.max(scores, axis=-1))
    weights = jnp.where(visible_wide, jnp.exp(scores - row_max[..., None]), 0.0)
    row_sum = lax.optimization_barrier(jnp.sum(weights, axis=-1))
    numerator = jnp.einsum('irj,jd->ird', lowered(weights), value_group.astype(jnp.float32), precision=lax.Precision.HIGHEST)
    return (numerator / row_sum[..., None], row_max + jnp.log(row_sum))

def group_backward(query_group, key_group, value_group, grad_group, visible):
    outputs, log_total = group_forward(query_group, key_group, value_group, visible)
    grad_wide = grad_group.astype(jnp.float32)
    delta_rows = lax.optimization_barrier(jnp.sum(grad_wide * outputs, axis=-1))
    visible_wide = visible[:, None, :]
    scores = group_scores(query_group, key_group)
    probabilities = jnp.where(visible_wide, jnp.exp(scores - log_total[..., None]), 0.0)
    value_part = jnp.einsum('irj,ird->jd', lowered(probabilities), grad_wide, precision=lax.Precision.HIGHEST)
    prob_grad = jnp.einsum('ird,jd->irj', grad_wide, value_group.astype(jnp.float32), precision=lax.Precision.HIGHEST)
    score_grad = lowered(probabilities * (prob_grad - delta_rows[..., None]))
    score_scale = 1.0 / math.sqrt(HEAD_DIM)
    query_part = jnp.einsum('irj,jd->ird', score_grad, key_group.astype(jnp.float32), precision=lax.Precision.HIGHEST) * score_scale
    key_part = jnp.einsum('irj,ird->jd', score_grad, query_group.astype(jnp.float32), precision=lax.Precision.HIGHEST) * score_scale
    return (query_part.astype(jnp.bfloat16), key_part.astype(jnp.bfloat16), value_part.astype(jnp.bfloat16))

def split_heads(query_section, key_section, value_section):
    group_ratio = HEADS // KV_HEADS
    query_split = query_section.reshape(SEQ, KV_HEADS, group_ratio, HEAD_DIM).transpose(1, 0, 2, 3)
    key_split = key_section.reshape(SEQ, KV_HEADS, HEAD_DIM).transpose(1, 0, 2)
    value_split = value_section.reshape(SEQ, KV_HEADS, HEAD_DIM).transpose(1, 0, 2)
    return (query_split, key_split, value_split)

def section_forward(section_items):
    query_section, key_section, value_section, seg_section = section_items
    visible = visible_pairs(seg_section)
    query_split, key_split, value_split = split_heads(query_section, key_section, value_section)

    def one_group(group_items):
        return group_forward(group_items[0], group_items[1], group_items[2], visible)[0]
    outputs = lax.map(one_group, (query_split, key_split, value_split))
    return outputs.transpose(1, 0, 2, 3).reshape(SEQ, HEADS * HEAD_DIM).astype(jnp.bfloat16)

def section_backward(section_items):
    query_section, key_section, value_section, seg_section, grad_section = section_items
    visible = visible_pairs(seg_section)
    query_split, key_split, value_split = split_heads(query_section, key_section, value_section)
    grad_split = grad_section.reshape(SEQ, KV_HEADS, HEADS // KV_HEADS, HEAD_DIM).transpose(1, 0, 2, 3)

    def one_group(group_items):
        return group_backward(group_items[0], group_items[1], group_items[2], group_items[3], visible)
    query_part, key_part, value_part = lax.map(one_group, (query_split, key_split, value_split, grad_split))
    query_grad = query_part.transpose(1, 0, 2, 3).reshape(SEQ, HEADS * HEAD_DIM)
    key_grad = key_part.transpose(1, 0, 2).reshape(SEQ, KV_HEADS * HEAD_DIM)
    value_grad = value_part.transpose(1, 0, 2).reshape(SEQ, KV_HEADS * HEAD_DIM)
    return (query_grad, key_grad, value_grad)

def reference(queries, key_rows, values, segments, held_queries, held_keys, held_values, held_segments, out_grad):
    attn_out = lax.map(section_forward, (queries, key_rows, values, segments))
    reloaded = (held_queries[::-1], held_keys[::-1], held_values[::-1], held_segments[::-1], out_grad)
    query_grad, key_grad, value_grad = lax.map(section_backward, reloaded)
    return (attn_out, query_grad, key_grad, value_grad)
```

```python
import functools
import math

import jax
import jax.numpy as jnp
from jax import lax
from jax.experimental import pallas as pl
from jax.experimental.pallas import tpu as pltpu
from jax.sharding import PartitionSpec as P

HEAD_DIM = 128
ROWS = 128
PIECES = 4
PIECE = ROWS // PIECES
HALO = 10
KEYS = HALO * ROWS
SPAN = 8
HIDDEN = -1e30
TO_LOG2 = math.log2(math.e) / math.sqrt(HEAD_DIM)
STEP = 256
VMEM_LIMIT = 48 * 1024 * 1024

SECTION_PAIRS = [(s, 7 - s) for s in range(8)]
FSDP_SWAP = [(f, f ^ 8) for f in range(16)]
FSDP_NINE = [(f, f + 9) for f in range(7)] + [(f + 9, f) for f in range(7)]
SECTION_FSDP_SWAP = [(s * 16 + f, (7 - s) * 16 + (f ^ 8)) for s in range(8) for f in range(16)]
ROW_GROUPS = [[z * 8 + y for y in range(8)] for z in range(2)]
ROW_TP_GROUPS = [[(z * 8 + y) * 4 + t for y in range(8) for t in range(4)] for z in range(2)]


def nt_dot(a, b):
    return lax.dot_general(a, b, (((1,), (1,)), ((), ())), preferred_element_type=jnp.float32)


def nn_dot(a, b):
    return jnp.dot(a, b, preferred_element_type=jnp.float32)


def write_bias(bias_ref, d, key_seg, query_seg, valid):
    key_wide = jnp.broadcast_to(key_seg, (ROWS, ROWS)).T
    seen = key_wide == jnp.broadcast_to(query_seg, (ROWS, ROWS))
    if d == 0:
        key_pos = lax.broadcasted_iota(jnp.int32, (ROWS, ROWS), 0)
        query_pos = lax.broadcasted_iota(jnp.int32, (ROWS, ROWS), 1)
        seen = seen & (key_pos <= query_pos)
        bias_ref[0:ROWS, :] = jnp.where(seen, 0.0, HIDDEN)
    else:
        shown = jnp.where(valid, 0.0, HIDDEN).astype(jnp.float32)
        bias_ref[d * ROWS : (d + 1) * ROWS, :] = jnp.where(seen, shown, HIDDEN)


def head_scores(keys_ref, bias_ref, scores_ref, query_pair):
    top = jnp.full((1, 2 * ROWS), HIDDEN, jnp.float32)
    for lo in range(0, KEYS, STEP):
        bias = bias_ref[lo : lo + STEP, :]
        raw = nt_dot(keys_ref[lo : lo + STEP, :], query_pair)
        scores = raw * TO_LOG2 + jnp.concatenate([bias, bias], axis=1)
        scores_ref[lo : lo + STEP, :] = scores
        top = jnp.maximum(top, jnp.max(scores, axis=0, keepdims=True))
    return top


def forward_kernel(f_ref, query_ref, gathered_ref, out_ref, keys, values_t, bias, scores):
    f = f_ref[0]
    upper = f >= SPAN
    for d in range(HALO):
        block = f - d
        valid = block >= 0
        block = jnp.maximum(block, 0)
        crossed = jnp.where(upper & (block < SPAN), 1, 0)
        entry = (block & (SPAN - 1)) * 2 + crossed
        keys[d * ROWS : (d + 1) * ROWS, :] = gathered_ref[entry, 0:ROWS, :]
        values_t[:, d * ROWS : (d + 1) * ROWS] = gathered_ref[entry, ROWS : 2 * ROWS, :].T
        key_seg = gathered_ref[entry, 2 * ROWS : 2 * ROWS + 16, :].astype(jnp.float32)[0:1]
        if d == 0:
            query_seg = key_seg
        write_bias(bias, d, key_seg, query_seg, valid)
    for pair in range(4):
        lo_col = pair * 2 * HEAD_DIM
        query_pair = jnp.concatenate(
            [query_ref[:, lo_col : lo_col + 128], query_ref[:, lo_col + 128 : lo_col + 256]], axis=0
        )
        top = head_scores(keys, bias, scores, query_pair)
        total = jnp.zeros((1, 2 * ROWS), jnp.float32)
        summed = jnp.zeros((HEAD_DIM, 2 * ROWS), jnp.float32)
        for lo in range(0, KEYS, STEP):
            weights = jnp.exp2(scores[lo : lo + STEP, :] - top)
            total = total + jnp.sum(weights, axis=0, keepdims=True)
            summed = summed + nn_dot(values_t[:, lo : lo + STEP], weights.astype(jnp.bfloat16))
        result = (summed / total).T.astype(jnp.bfloat16)
        out_ref[:, lo_col : lo_col + 128] = result[0:128]
        out_ref[:, lo_col + 128 : lo_col + 256] = result[128:256]


def backward_kernel(
    f_ref,
    own_ref,
    slots_ref,
    nine_ref,
    grad_ref,
    query_grad_ref,
    send_ref,
    send_nine_ref,
    own_part_ref,
    keys,
    keys_t,
    values,
    bias,
    scores,
    prob_grads,
    key_sum,
    value_sum,
):
    f = f_ref[0]
    y = f & (SPAN - 1)
    upper = f >= SPAN
    for d in range(HALO):
        base = d * ROWS
        slot = (y - d) & (SPAN - 1)
        for piece in range(PIECES):
            at = base + piece * PIECE
            if d == 0:
                key_piece = own_ref[piece, :, 1024:1152]
                value_piece = own_ref[piece, :, 1152:1280]
            elif d == HALO - 1:
                key_piece = nine_ref[piece, :, 0:128]
                value_piece = nine_ref[piece, :, 128:256]
            else:
                key_piece = slots_ref[slot * PIECES + piece, 0:PIECE, :]
                value_piece = slots_ref[slot * PIECES + piece, PIECE : 2 * PIECE, :]
            keys[at : at + PIECE, :] = key_piece
            values[at : at + PIECE, :] = value_piece
        keys_t[:, base : base + ROWS] = keys[base : base + ROWS, :].T
        ids = slots_ref[slot * PIECES, 2 * PIECE : 2 * PIECE + 16, :].astype(jnp.float32)
        if d == 0:
            query_seg = ids[1:2]
            key_seg = query_seg
        elif d == HALO - 1:
            key_seg = ids[2:3]
        else:
            key_seg = ids[0:1]
        valid = (f >= d) if d < HALO - 1 else (upper & (y >= 1))
        write_bias(bias, d, key_seg, query_seg, valid)
    for pair in range(4):
        lo_col = pair * 2 * HEAD_DIM
        query_pair = jnp.concatenate(
            [
                own_ref[piece, :, col : col + 128]
                for col in (lo_col, lo_col + 128)
                for piece in range(PIECES)
            ],
            axis=0,
        )
        grad_pair = jnp.concatenate(
            [grad_ref[:, lo_col : lo_col + 128], grad_ref[:, lo_col + 128 : lo_col + 256]], axis=0
        )
        top = head_scores(keys, bias, scores, query_pair)
        total = jnp.zeros((1, 2 * ROWS), jnp.float32)
        mixed = jnp.zeros((1, 2 * ROWS), jnp.float32)
        for lo in range(0, KEYS, STEP):
            weights = jnp.exp2(scores[lo : lo + STEP, :] - top)
            prob_grad = nt_dot(values[lo : lo + STEP, :], grad_pair)
            total = total + jnp.sum(weights, axis=0, keepdims=True)
            mixed = mixed + jnp.sum(weights * prob_grad, axis=0, keepdims=True)
            scores[lo : lo + STEP, :] = weights
            prob_grads[lo : lo + STEP, :] = prob_grad
        inverse = 1.0 / total
        delta = mixed * inverse
        query_sum = jnp.zeros((HEAD_DIM, 2 * ROWS), jnp.float32)
        for lo in range(0, KEYS, STEP):
            probabilities = scores[lo : lo + STEP, :] * inverse
            score_grad = (probabilities * (prob_grads[lo : lo + STEP, :] - delta)).astype(
                jnp.bfloat16
            )
            value_part = nn_dot(probabilities.astype(jnp.bfloat16), grad_pair)
            key_part = nn_dot(score_grad, query_pair)
            query_sum = query_sum + nn_dot(keys_t[:, lo : lo + STEP], score_grad)
            if pair == 0:
                value_sum[lo : lo + STEP, :] = value_part
                key_sum[lo : lo + STEP, :] = key_part
            else:
                value_sum[lo : lo + STEP, :] += value_part
                key_sum[lo : lo + STEP, :] += key_part
        result = (query_sum * (1.0 / math.sqrt(HEAD_DIM))).T.astype(jnp.bfloat16)
        query_grad_ref[:, lo_col : lo_col + 128] = result[0:128]
        query_grad_ref[:, lo_col + 128 : lo_col + 256] = result[128:256]
    own_part_ref[0:ROWS, :] = key_sum[0:ROWS, :]
    own_part_ref[ROWS : 2 * ROWS, :] = value_sum[0:ROWS, :]
    for d in range(1, HALO):
        key_out = key_sum[d * ROWS : (d + 1) * ROWS, :].astype(jnp.bfloat16)
        value_out = value_sum[d * ROWS : (d + 1) * ROWS, :].astype(jnp.bfloat16)
        if d == HALO - 1:
            send_nine_ref[0:ROWS, :] = key_out
            send_nine_ref[ROWS : 2 * ROWS, :] = value_out
        else:
            slot = (y - d) & (SPAN - 1)
            send_ref[slot, 0:ROWS, :] = key_out
            send_ref[slot, ROWS : 2 * ROWS, :] = value_out


VMEM = pl.BlockSpec(memory_space=pltpu.VMEM)
SMEM = pl.BlockSpec(memory_space=pltpu.SMEM)


def run_forward(f, query, gathered):
    return pl.pallas_call(
        forward_kernel,
        out_shape=jax.ShapeDtypeStruct((ROWS, 1024), jnp.bfloat16),
        in_specs=[SMEM, VMEM, VMEM],
        out_specs=VMEM,
        scratch_shapes=[
            pltpu.VMEM((KEYS, HEAD_DIM), jnp.bfloat16),
            pltpu.VMEM((HEAD_DIM, KEYS), jnp.bfloat16),
            pltpu.VMEM((KEYS, ROWS), jnp.float32),
            pltpu.VMEM((KEYS, 2 * ROWS), jnp.float32),
        ],
        compiler_params=pltpu.CompilerParams(vmem_limit_bytes=VMEM_LIMIT),
        cost_estimate=pl.CostEstimate(
            flops=2 * 2 * 1024 * KEYS * 128, bytes_accessed=3_000_000, transcendentals=1024 * KEYS
        ),
        name="forward_attention",
    )(f, query, gathered)


def run_backward(f, own, slots, nine, grad):
    return pl.pallas_call(
        backward_kernel,
        out_shape=(
            jax.ShapeDtypeStruct((ROWS, 1024), jnp.bfloat16),
            jax.ShapeDtypeStruct((SPAN, 2 * ROWS, HEAD_DIM), jnp.bfloat16),
            jax.ShapeDtypeStruct((2 * ROWS, HEAD_DIM), jnp.bfloat16),
            jax.ShapeDtypeStruct((2 * ROWS, HEAD_DIM), jnp.float32),
        ),
        in_specs=[SMEM, VMEM, VMEM, VMEM, VMEM],
        out_specs=(VMEM, VMEM, VMEM, VMEM),
        scratch_shapes=[
            pltpu.VMEM((KEYS, HEAD_DIM), jnp.bfloat16),
            pltpu.VMEM((HEAD_DIM, KEYS), jnp.bfloat16),
            pltpu.VMEM((KEYS, HEAD_DIM), jnp.bfloat16),
            pltpu.VMEM((KEYS, ROWS), jnp.float32),
            pltpu.VMEM((KEYS, 2 * ROWS), jnp.float32),
            pltpu.VMEM((KEYS, 2 * ROWS), jnp.float32),
            pltpu.VMEM((KEYS, HEAD_DIM), jnp.float32),
            pltpu.VMEM((KEYS, HEAD_DIM), jnp.float32),
        ],
        compiler_params=pltpu.CompilerParams(vmem_limit_bytes=VMEM_LIMIT),
        cost_estimate=pl.CostEstimate(
            flops=5 * 2 * 1024 * KEYS * 128, bytes_accessed=4_000_000, transcendentals=1024 * KEYS
        ),
        name="backward_attention",
    )(f, own, slots, nine, grad)


def local(
    queries,
    key_rows,
    values,
    segments,
    held_queries,
    held_keys,
    held_values,
    held_segments,
    out_grad,
):
    f = lax.axis_index("fsdp").astype(jnp.int32)
    y = f & (SPAN - 1)
    upper = f >= SPAN
    f_arr = f.reshape(1)

    stash = jnp.concatenate(
        [
            held_queries[0].reshape(PIECE, 4, 1024),
            held_keys[0].reshape(PIECE, 4, 128),
            held_values[0].reshape(PIECE, 4, 128),
        ],
        axis=2,
    ).transpose(1, 0, 2)
    stash = lax.all_to_all(stash, "tp", split_axis=0, concat_axis=0, tiled=False)
    own = lax.ppermute(stash, "section", SECTION_PAIRS)

    held_ids = held_segments[0].astype(jnp.bfloat16)
    token_cut = jnp.concatenate(
        [
            held_keys[0].reshape(PIECE, 4, 128).transpose(1, 0, 2),
            held_values[0].reshape(PIECE, 4, 128).transpose(1, 0, 2),
            jnp.broadcast_to(held_ids[None, None, :], (4, 16, 128)),
        ],
        axis=1,
    )
    straight = lax.ppermute(token_cut, "section", SECTION_PAIRS)
    crossed = lax.ppermute(token_cut, ("section", "fsdp"), SECTION_FSDP_SWAP)
    id_rows = lax.broadcasted_iota(jnp.int32, (4, 16, 128), 1)
    target = lax.broadcasted_iota(jnp.int32, (SPAN, 1, 1, 1), 0)
    take_crossed = (target <= y) & upper
    body = jnp.where(take_crossed, crossed[None, :, : 2 * PIECE], straight[None, :, : 2 * PIECE])
    straight_ids = straight[None, :, 2 * PIECE :]
    crossed_ids = crossed[None, :, 2 * PIECE :]
    ids = jnp.where(take_crossed, crossed_ids, straight_ids)
    ids = jnp.where(id_rows[None] == 1, straight_ids, jnp.where(id_rows[None] == 2, crossed_ids, ids))
    outgoing = jnp.concatenate([body, ids], axis=2).reshape(SPAN * 4, 2 * PIECE + 16, 128)
    slots = lax.all_to_all(
        outgoing,
        ("fsdp", "tp"),
        split_axis=0,
        concat_axis=0,
        tiled=False,
        axis_index_groups=ROW_TP_GROUPS,
    )
    nine = lax.ppermute(own[:, :, 1024:], "fsdp", FSDP_NINE)

    ids_low = segments[0].astype(jnp.bfloat16)
    forward_part = jnp.concatenate(
        [key_rows[0], values[0], jnp.broadcast_to(ids_low[None, :], (16, 128))], axis=0
    )
    forward_cross = lax.ppermute(forward_part, "fsdp", FSDP_SWAP)
    gathered = lax.all_gather(
        jnp.stack([forward_part, forward_cross]),
        "fsdp",
        axis=0,
        tiled=True,
        axis_index_groups=ROW_GROUPS,
    )

    query_grad, send, send_nine, own_part = run_backward(f_arr, own, slots, nine, out_grad[0])
    parts = lax.all_to_all(
        send, "fsdp", split_axis=0, concat_axis=0, tiled=False, axis_index_groups=ROW_GROUPS
    )
    from_nine = lax.ppermute(send_nine, "fsdp", FSDP_NINE)
    attn_out = run_forward(f_arr, queries[0], gathered)

    source = lax.broadcasted_iota(jnp.int32, (SPAN, 1, 1), 0)
    parts_wide = parts.astype(jnp.float32)
    same_row = jnp.sum(jnp.where(source > y, parts_wide, 0.0), axis=0) + own_part
    other_row = jnp.sum(jnp.where(source <= y, parts_wide, 0.0), axis=0).astype(jnp.bfloat16)
    from_upper = lax.ppermute(other_row, "fsdp", FSDP_SWAP)
    late = from_upper.astype(jnp.float32) + from_nine.astype(jnp.float32)
    final = same_row + jnp.where(upper, 0.0, late)
    key_grad = (final[:ROWS] * (1.0 / math.sqrt(HEAD_DIM))).astype(jnp.bfloat16)
    value_grad = final[ROWS:].astype(jnp.bfloat16)
    return (attn_out[None], query_grad[None], key_grad[None], value_grad[None])


def solution(mesh):
    return jax.shard_map(
        local,
        mesh=mesh,
        in_specs=(
            P("section", "fsdp", "tp"),
            P("section", "fsdp", "tp"),
            P("section", "fsdp", "tp"),
            P("section", "fsdp"),
            P("section", ("fsdp", "tp"), None),
            P("section", ("fsdp", "tp"), None),
            P("section", ("fsdp", "tp"), None),
            P("section", "fsdp"),
            P("section", "fsdp", "tp"),
        ),
        out_specs=(
            P("section", "fsdp", "tp"),
            P("section", "fsdp", "tp"),
            P("section", "fsdp", "tp"),
            P("section", "fsdp", "tp"),
        ),
        check_vma=False,
    )
```

```python
import functools
import math

import jax
import jax.numpy as jnp
from jax import lax
from jax.experimental import pallas as pl
from jax.experimental.pallas import tpu as pltpu
from jax.sharding import PartitionSpec as P

HEAD_DIM = 128
ROWS = 128
PIECES = 4
PIECE = ROWS // PIECES
HALO = 10
KEYS = HALO * ROWS
SPAN = 8
HIDDEN = -1e30
TO_LOG2 = math.log2(math.e) / math.sqrt(HEAD_DIM)
STEP = 256
VMEM_LIMIT = 24 * 1024 * 1024
SMALL_LIMIT = 8 * 1024 * 1024

BLOCK = 2 * ROWS + 16
CUT = 2 * PIECE + 8

FSDP_SWAP = [(f, f ^ 8) for f in range(16)]
FSDP_NINE = [(f, f + 9) for f in range(7)] + [(f + 9, f) for f in range(7)]
SECTION_PAIRS = [(s, 7 - s) for s in range(8)]
TP_ROUTES = [[(t, t ^ d) for t in range(4)] for d in range(4)]
MIRROR_GROUPS = [
    [(s * 16 + z * 8 + y) * 4 + t for s in (k, 7 - k) for z in range(2) for t in range(4)]
    for k in range(4)
    for y in range(8)
]
ROW_GROUPS = [[z * 8 + y for y in range(8)] for z in range(2)]


def fsdp_place():
    f = lax.axis_index("fsdp").astype(jnp.int32)
    return f, f & (SPAN - 1), f >= SPAN


def nt_dot(a, b):
    return lax.dot_general(a, b, (((1,), (1,)), ((), ())), preferred_element_type=jnp.float32)


def nn_dot(a, b):
    return jnp.dot(a, b, preferred_element_type=jnp.float32)


def write_bias(bias_ref, d, key_seg, query_seg, valid):
    key_wide = jnp.broadcast_to(key_seg, (ROWS, ROWS)).T
    seen = key_wide == jnp.broadcast_to(query_seg, (ROWS, ROWS))
    if d == 0:
        key_pos = lax.broadcasted_iota(jnp.int32, (ROWS, ROWS), 0)
        query_pos = lax.broadcasted_iota(jnp.int32, (ROWS, ROWS), 1)
        seen = seen & (key_pos <= query_pos)
        bias_ref[0:ROWS, :] = jnp.where(seen, 0.0, HIDDEN)
    else:
        shown = jnp.where(valid, 0.0, HIDDEN).astype(jnp.float32)
        bias_ref[d * ROWS : (d + 1) * ROWS, :] = jnp.where(seen, shown, HIDDEN)


def head_scores(keys_ref, bias_ref, scores_ref, query_pair):
    top = jnp.full((1, 2 * ROWS), HIDDEN, jnp.float32)
    for lo in range(0, KEYS, STEP):
        bias = bias_ref[lo : lo + STEP, :]
        raw = nt_dot(keys_ref[lo : lo + STEP, :], query_pair)
        scores = raw * TO_LOG2 + jnp.concatenate([bias, bias], axis=1)
        scores_ref[lo : lo + STEP, :] = scores
        top = jnp.maximum(top, jnp.max(scores, axis=0, keepdims=True))
    return top


def forward_kernel(query_ref, gathered_ref, out_ref, keys, values_t, bias, scores):
    f, y, upper = fsdp_place()
    for d in range(HALO):
        valid = f >= d
        block = jnp.maximum(f - d, 0)
        crossed = jnp.where(upper & (block < SPAN), 1, 0)
        entry = (block & (SPAN - 1)) * 2 + crossed
        keys[d * ROWS : (d + 1) * ROWS, :] = gathered_ref[entry, 0:ROWS, :]
        values_t[:, d * ROWS : (d + 1) * ROWS] = gathered_ref[entry, ROWS : 2 * ROWS, :].T
        key_seg = gathered_ref[entry, 2 * ROWS : 2 * ROWS + 16, :].astype(jnp.float32)[0:1]
        if d == 0:
            query_seg = key_seg
        write_bias(bias, d, key_seg, query_seg, valid)
    for pair in range(4):
        lo_col = pair * 2 * HEAD_DIM
        query_pair = jnp.concatenate(
            [query_ref[:, lo_col : lo_col + 128], query_ref[:, lo_col + 128 : lo_col + 256]], axis=0
        )
        top = head_scores(keys, bias, scores, query_pair)
        total = jnp.zeros((1, 2 * ROWS), jnp.float32)
        summed = jnp.zeros((HEAD_DIM, 2 * ROWS), jnp.float32)
        for lo in range(0, KEYS, STEP):
            weights = jnp.exp2(scores[lo : lo + STEP, :] - top)
            total = total + jnp.sum(weights, axis=0, keepdims=True)
            summed = summed + nn_dot(values_t[:, lo : lo + STEP], weights.astype(jnp.bfloat16))
        result = (summed / total).T.astype(jnp.bfloat16)
        out_ref[:, lo_col : lo_col + 128] = result[0:128]
        out_ref[:, lo_col + 128 : lo_col + 256] = result[128:256]


def backward_kernel(
    query_0_ref,
    query_1_ref,
    query_2_ref,
    query_3_ref,
    own_ref,
    slots_ref,
    nine_ref,
    grad_ref,
    query_grad_ref,
    send_ref,
    send_nine_ref,
    own_part_ref,
    queries,
    keys,
    keys_t,
    values,
    bias,
    scores,
    prob_grads,
    key_sum,
    value_sum,
):
    f, y, upper = fsdp_place()
    t = lax.axis_index("tp").astype(jnp.int32)
    for apart, ref in enumerate((query_0_ref, query_1_ref, query_2_ref, query_3_ref)):
        at = pl.multiple_of((t ^ apart) * PIECE, PIECE)
        queries[pl.ds(at, PIECE), :] = ref[...]
    for d in range(HALO):
        base = d * ROWS
        if d == 0:
            block = own_ref[...]
            valid = True
        elif d == HALO - 1:
            block = nine_ref[...]
            valid = upper & (y >= 1)
        else:
            block = slots_ref[(y - d) & (SPAN - 1)]
            valid = f >= d
        keys[base : base + ROWS, :] = block[0:ROWS]
        values[base : base + ROWS, :] = block[ROWS : 2 * ROWS]
        keys_t[:, base : base + ROWS] = block[0:ROWS].T
        key_seg = block[2 * ROWS :].astype(jnp.float32)[0:1]
        if d == 0:
            query_seg = key_seg
        write_bias(bias, d, key_seg, query_seg, valid)
    for pair in range(4):
        lo_col = pair * 2 * HEAD_DIM
        query_pair = jnp.concatenate(
            [queries[:, lo_col : lo_col + 128], queries[:, lo_col + 128 : lo_col + 256]], axis=0
        )
        grad_pair = jnp.concatenate(
            [grad_ref[:, lo_col : lo_col + 128], grad_ref[:, lo_col + 128 : lo_col + 256]], axis=0
        )
        top = head_scores(keys, bias, scores, query_pair)
        total = jnp.zeros((1, 2 * ROWS), jnp.float32)
        mixed = jnp.zeros((1, 2 * ROWS), jnp.float32)
        for lo in range(0, KEYS, STEP):
            weights = jnp.exp2(scores[lo : lo + STEP, :] - top)
            prob_grad = nt_dot(values[lo : lo + STEP, :], grad_pair)
            total = total + jnp.sum(weights, axis=0, keepdims=True)
            mixed = mixed + jnp.sum(weights * prob_grad, axis=0, keepdims=True)
            scores[lo : lo + STEP, :] = weights
            prob_grads[lo : lo + STEP, :] = prob_grad
        inverse = 1.0 / total
        delta = mixed * inverse
        query_sum = jnp.zeros((HEAD_DIM, 2 * ROWS), jnp.float32)
        for lo in range(0, KEYS, STEP):
            probabilities = scores[lo : lo + STEP, :] * inverse
            score_grad = (probabilities * (prob_grads[lo : lo + STEP, :] - delta)).astype(
                jnp.bfloat16
            )
            value_part = nn_dot(probabilities.astype(jnp.bfloat16), grad_pair)
            key_part = nn_dot(score_grad, query_pair)
            query_sum = query_sum + nn_dot(keys_t[:, lo : lo + STEP], score_grad)
            if pair == 0:
                value_sum[lo : lo + STEP, :] = value_part
                key_sum[lo : lo + STEP, :] = key_part
            else:
                value_sum[lo : lo + STEP, :] += value_part
                key_sum[lo : lo + STEP, :] += key_part
        result = (query_sum * (1.0 / math.sqrt(HEAD_DIM))).T.astype(jnp.bfloat16)
        query_grad_ref[:, lo_col : lo_col + 128] = result[0:128]
        query_grad_ref[:, lo_col + 128 : lo_col + 256] = result[128:256]
    own_part_ref[0:ROWS, :] = key_sum[0:ROWS, :]
    own_part_ref[ROWS : 2 * ROWS, :] = value_sum[0:ROWS, :]
    for d in range(1, HALO):
        key_out = key_sum[d * ROWS : (d + 1) * ROWS, :].astype(jnp.bfloat16)
        value_out = value_sum[d * ROWS : (d + 1) * ROWS, :].astype(jnp.bfloat16)
        if d == HALO - 1:
            send_nine_ref[0:ROWS, :] = key_out
            send_nine_ref[ROWS : 2 * ROWS, :] = value_out
        else:
            slot = (y - d) & (SPAN - 1)
            send_ref[slot, 0:ROWS, :] = key_out
            send_ref[slot, ROWS : 2 * ROWS, :] = value_out


VMEM = pl.BlockSpec(memory_space=pltpu.VMEM)
ANY = pl.BlockSpec(memory_space=pl.ANY)


def wide_ids(ids_ref):
    return jnp.broadcast_to(ids_ref[...].astype(jnp.float32), (16, 128)).astype(jnp.bfloat16)


def prepare_kernel(
    held_key_ref, held_value_ref, held_ids_ref, key_ref, value_ref, ids_ref, cut_ref, forward_ref
):
    held_ids = wide_ids(held_ids_ref)[0:8]
    for t in range(PIECES):
        cut = jnp.concatenate(
            [
                held_key_ref[0, :, t * 128 : (t + 1) * 128],
                held_value_ref[0, :, t * 128 : (t + 1) * 128],
                held_ids,
            ],
            axis=0,
        )
        for copy in range(4):
            cut_ref[copy * PIECES + t] = cut
    forward_ref[0:ROWS, :] = key_ref[0]
    forward_ref[ROWS : 2 * ROWS, :] = value_ref[0]
    forward_ref[2 * ROWS :, :] = wide_ids(ids_ref)


def outgoing_kernel(
    cuts_ref, query_ref, forward_ref, forward_cross_ref, own_ref, outgoing_ref, stacked_ref, *part_refs
):
    f, y, upper = fsdp_place()
    t = lax.axis_index("tp").astype(jnp.int32)
    for apart, ref in enumerate(part_refs):
        lo = pl.multiple_of((t ^ apart) * 1024, 1024)
        ref[...] = query_ref[:, pl.ds(lo, 1024)]
    side = jnp.where(lax.axis_index("section") < 4, 2 * PIECES, 0)
    row = jnp.where(upper, PIECES, 0)

    def whole(first):
        cuts = [cuts_ref[first + piece] for piece in range(PIECES)]
        ids = cuts[0][2 * PIECE :]
        return jnp.concatenate(
            [cut[:PIECE] for cut in cuts] + [cut[PIECE : 2 * PIECE] for cut in cuts] + [ids, ids],
            axis=0,
        )

    own = whole(side + row)
    crossed = whole(side + PIECES - row)
    own_ref[...] = own
    for target in range(SPAN):
        outgoing_ref[target] = jnp.where(upper & (target <= y), crossed, own)
    stacked_ref[0] = forward_ref[...]
    stacked_ref[1] = forward_cross_ref[...]


def run_small(kernel, name, limit, shapes, *arrays, waits=()):
    return pl.pallas_call(
        kernel,
        out_shape=tuple(jax.ShapeDtypeStruct(shape, jnp.bfloat16) for shape in shapes),
        in_specs=[VMEM] * len(arrays) + [ANY] * len(waits),
        out_specs=(VMEM,) * len(shapes),
        compiler_params=pltpu.CompilerParams(vmem_limit_bytes=limit) if limit else None,
        name=name,
    )(*arrays, *waits)


def run_forward(query, gathered):
    return pl.pallas_call(
        forward_kernel,
        out_shape=jax.ShapeDtypeStruct((ROWS, 1024), jnp.bfloat16),
        in_specs=[VMEM, VMEM],
        out_specs=VMEM,
        scratch_shapes=[
            pltpu.VMEM((KEYS, HEAD_DIM), jnp.bfloat16),
            pltpu.VMEM((HEAD_DIM, KEYS), jnp.bfloat16),
            pltpu.VMEM((KEYS, ROWS), jnp.float32),
            pltpu.VMEM((KEYS, 2 * ROWS), jnp.float32),
        ],
        compiler_params=pltpu.CompilerParams(vmem_limit_bytes=VMEM_LIMIT),
        cost_estimate=pl.CostEstimate(
            flops=2 * 2 * 1024 * KEYS * 128, bytes_accessed=3_000_000, transcendentals=1024 * KEYS
        ),
        name="forward_attention",
    )(query, gathered)


def run_backward(queries, own, slots, nine, grad):
    return pl.pallas_call(
        backward_kernel,
        out_shape=(
            jax.ShapeDtypeStruct((ROWS, 1024), jnp.bfloat16),
            jax.ShapeDtypeStruct((SPAN, 2 * ROWS, HEAD_DIM), jnp.bfloat16),
            jax.ShapeDtypeStruct((2 * ROWS, HEAD_DIM), jnp.bfloat16),
            jax.ShapeDtypeStruct((2 * ROWS, HEAD_DIM), jnp.float32),
        ),
        in_specs=[VMEM] * 8,
        out_specs=(VMEM, VMEM, VMEM, VMEM),
        scratch_shapes=[
            pltpu.VMEM((ROWS, 1024), jnp.bfloat16),
            pltpu.VMEM((KEYS, HEAD_DIM), jnp.bfloat16),
            pltpu.VMEM((HEAD_DIM, KEYS), jnp.bfloat16),
            pltpu.VMEM((KEYS, HEAD_DIM), jnp.bfloat16),
            pltpu.VMEM((KEYS, ROWS), jnp.float32),
            pltpu.VMEM((KEYS, 2 * ROWS), jnp.float32),
            pltpu.VMEM((KEYS, 2 * ROWS), jnp.float32),
            pltpu.VMEM((KEYS, HEAD_DIM), jnp.float32),
            pltpu.VMEM((KEYS, HEAD_DIM), jnp.float32),
        ],
        compiler_params=pltpu.CompilerParams(vmem_limit_bytes=VMEM_LIMIT),
        cost_estimate=pl.CostEstimate(
            flops=5 * 2 * 1024 * KEYS * 128, bytes_accessed=4_000_000, transcendentals=1024 * KEYS
        ),
        name="backward_attention",
    )(*queries, own, slots, nine, grad)


def local(
    queries,
    key_rows,
    values,
    segments,
    held_queries,
    held_keys,
    held_values,
    held_segments,
    out_grad,
):
    f = lax.axis_index("fsdp").astype(jnp.int32)
    y = f & (SPAN - 1)
    upper = f >= SPAN
    query_back = lax.ppermute(held_queries[0], "section", SECTION_PAIRS)
    cuts, forward_part = run_small(
        prepare_kernel,
        "prepare",
        None,
        ((4 * PIECES, CUT, 128), (BLOCK, 128)),
        held_keys,
        held_values,
        held_segments,
        key_rows,
        values,
        segments,
    )
    cuts = lax.all_to_all(
        cuts,
        ("section", "fsdp", "tp"),
        split_axis=0,
        concat_axis=0,
        tiled=False,
        axis_index_groups=MIRROR_GROUPS,
    )
    forward_cross = lax.ppermute(forward_part, "fsdp", FSDP_SWAP)
    own, outgoing, stacked, *parts = run_small(
        outgoing_kernel,
        "outgoing",
        SMALL_LIMIT,
        ((BLOCK, 128), (SPAN, BLOCK, 128), (2, BLOCK, 128), *[(PIECE, 1024)] * 4),
        cuts,
        query_back,
        forward_part,
        forward_cross,
    )
    stash = [parts[0]] + [lax.ppermute(parts[d], "tp", TP_ROUTES[d]) for d in (1, 2, 3)]
    slots = lax.all_to_all(
        outgoing, "fsdp", split_axis=0, concat_axis=0, tiled=False, axis_index_groups=ROW_GROUPS
    )
    nine = lax.ppermute(own, "fsdp", FSDP_NINE)
    gathered = lax.all_gather(
        stacked, "fsdp", axis=0, tiled=True, axis_index_groups=ROW_GROUPS
    )

    query_grad, send, send_nine, own_part = run_backward(stash, own, slots, nine, out_grad[0])
    parts = lax.all_to_all(
        send, "fsdp", split_axis=0, concat_axis=0, tiled=False, axis_index_groups=ROW_GROUPS
    )
    from_nine = lax.ppermute(send_nine, "fsdp", FSDP_NINE)
    attn_out = run_forward(queries[0], gathered)

    source = lax.broadcasted_iota(jnp.int32, (SPAN, 1, 1), 0)
    parts_wide = parts.astype(jnp.float32)
    same_row = jnp.sum(jnp.where(source > y, parts_wide, 0.0), axis=0) + own_part
    other_row = jnp.sum(jnp.where(source <= y, parts_wide, 0.0), axis=0).astype(jnp.bfloat16)
    from_upper = lax.ppermute(other_row, "fsdp", FSDP_SWAP)
    late = from_upper.astype(jnp.float32) + from_nine.astype(jnp.float32)
    final = same_row + jnp.where(upper, 0.0, late)
    key_grad = (final[:ROWS] * (1.0 / math.sqrt(HEAD_DIM))).astype(jnp.bfloat16)
    value_grad = final[ROWS:].astype(jnp.bfloat16)
    return (attn_out[None], query_grad[None], key_grad[None], value_grad[None])


def solution(mesh):
    return jax.shard_map(
        local,
        mesh=mesh,
        in_specs=(
            P("section", "fsdp", "tp"),
            P("section", "fsdp", "tp"),
            P("section", "fsdp", "tp"),
            P("section", "fsdp"),
            P("section", ("fsdp", "tp"), None),
            P("section", ("fsdp", "tp"), None),
            P("section", ("fsdp", "tp"), None),
            P("section", "fsdp"),
            P("section", "fsdp", "tp"),
        ),
        out_specs=(
            P("section", "fsdp", "tp"),
            P("section", "fsdp", "tp"),
            P("section", "fsdp", "tp"),
            P("section", "fsdp", "tp"),
        ),
        check_vma=False,
    )
```

```python
import functools
import math

import jax
import jax.numpy as jnp
from jax import lax
from jax.experimental import pallas as pl
from jax.experimental.pallas import tpu as pltpu
from jax.sharding import PartitionSpec as P

HEAD_DIM = 128
ROWS = 128
PIECES = 4
PIECE = ROWS // PIECES
HALO = 10
KEYS = HALO * ROWS
SPAN = 8
HIDDEN = -1e30
TO_LOG2 = math.log2(math.e) / math.sqrt(HEAD_DIM)
STEP = 256
VMEM_LIMIT = 24 * 1024 * 1024
SMALL_LIMIT = 8 * 1024 * 1024

BLOCK = 2 * ROWS + 16
CUT = 2 * PIECE + 8

FSDP_SWAP = [(f, f ^ 8) for f in range(16)]
FSDP_NINE = [(f, f + 9) for f in range(7)] + [(f + 9, f) for f in range(7)]
SECTION_PAIRS = [(s, 7 - s) for s in range(8)]
TP_ROUTES = [[(t, t ^ d) for t in range(4)] for d in range(4)]
MIRROR_GROUPS = [
    [(s * 16 + z * 8 + y) * 4 + t for s in (k, 7 - k) for z in range(2) for t in range(4)]
    for k in range(4)
    for y in range(8)
]
ROW_GROUPS = [[z * 8 + y for y in range(8)] for z in range(2)]


def fsdp_place():
    f = lax.axis_index("fsdp").astype(jnp.int32)
    return f, f & (SPAN - 1), f >= SPAN


def nt_dot(a, b):
    return lax.dot_general(a, b, (((1,), (1,)), ((), ())), preferred_element_type=jnp.float32)


def nn_dot(a, b):
    return jnp.dot(a, b, preferred_element_type=jnp.float32)


def write_bias(bias_ref, d, key_seg, query_seg, valid):
    key_wide = jnp.broadcast_to(key_seg, (ROWS, ROWS)).T
    seen = key_wide == jnp.broadcast_to(query_seg, (ROWS, ROWS))
    if d == 0:
        key_pos = lax.broadcasted_iota(jnp.int32, (ROWS, ROWS), 0)
        query_pos = lax.broadcasted_iota(jnp.int32, (ROWS, ROWS), 1)
        seen = seen & (key_pos <= query_pos)
        bias_ref[0:ROWS, :] = jnp.where(seen, 0.0, HIDDEN)
    else:
        shown = jnp.where(valid, 0.0, HIDDEN).astype(jnp.float32)
        bias_ref[d * ROWS : (d + 1) * ROWS, :] = jnp.where(seen, shown, HIDDEN)


def head_scores(keys_ref, bias_ref, scores_ref, query_pair):
    top = jnp.full((1, 2 * ROWS), HIDDEN, jnp.float32)
    for lo in range(0, KEYS, STEP):
        bias = bias_ref[lo : lo + STEP, :]
        raw = nt_dot(keys_ref[lo : lo + STEP, :], query_pair)
        scores = raw * TO_LOG2 + jnp.concatenate([bias, bias], axis=1)
        scores_ref[lo : lo + STEP, :] = scores
        top = jnp.maximum(top, jnp.max(scores, axis=0, keepdims=True))
    return top


def forward_kernel(query_ref, gathered_ref, out_ref, mark_ref, keys, values_t, bias, scores):
    f, y, upper = fsdp_place()
    for d in range(HALO):
        valid = f >= d
        block = jnp.maximum(f - d, 0)
        crossed = jnp.where(upper & (block < SPAN), 1, 0)
        entry = (block & (SPAN - 1)) * 2 + crossed
        keys[d * ROWS : (d + 1) * ROWS, :] = gathered_ref[entry, 0:ROWS, :]
        values_t[:, d * ROWS : (d + 1) * ROWS] = gathered_ref[entry, ROWS : 2 * ROWS, :].T
        key_seg = gathered_ref[entry, 2 * ROWS : 2 * ROWS + 16, :].astype(jnp.float32)[0:1]
        if d == 0:
            query_seg = key_seg
        write_bias(bias, d, key_seg, query_seg, valid)
    for pair in range(4):
        lo_col = pair * 2 * HEAD_DIM
        query_pair = jnp.concatenate(
            [query_ref[:, lo_col : lo_col + 128], query_ref[:, lo_col + 128 : lo_col + 256]], axis=0
        )
        top = head_scores(keys, bias, scores, query_pair)
        total = jnp.zeros((1, 2 * ROWS), jnp.float32)
        summed = jnp.zeros((HEAD_DIM, 2 * ROWS), jnp.float32)
        for lo in range(0, KEYS, STEP):
            weights = jnp.exp2(scores[lo : lo + STEP, :] - top)
            total = total + jnp.sum(weights, axis=0, keepdims=True)
            summed = summed + nn_dot(values_t[:, lo : lo + STEP], weights.astype(jnp.bfloat16))
        result = (summed / total).T.astype(jnp.bfloat16)
        out_ref[:, lo_col : lo_col + 128] = result[0:128]
        out_ref[:, lo_col + 128 : lo_col + 256] = result[128:256]
    mark_ref[...] = jnp.zeros((8, 128), jnp.float32)


def backward_kernel(
    query_0_ref,
    query_1_ref,
    query_2_ref,
    query_3_ref,
    own_ref,
    slots_ref,
    nine_ref,
    grad_ref,
    query_grad_ref,
    send_ref,
    send_nine_ref,
    own_part_ref,
    queries,
    keys,
    keys_t,
    values,
    bias,
    scores,
    prob_grads,
    key_sum,
    value_sum,
):
    f, y, upper = fsdp_place()
    t = lax.axis_index("tp").astype(jnp.int32)
    for apart, ref in enumerate((query_0_ref, query_1_ref, query_2_ref, query_3_ref)):
        at = pl.multiple_of((t ^ apart) * PIECE, PIECE)
        queries[pl.ds(at, PIECE), :] = ref[...]
    for d in range(HALO):
        base = d * ROWS
        if d == 0:
            block = own_ref[...]
            valid = True
        elif d == HALO - 1:
            block = nine_ref[...]
            valid = upper & (y >= 1)
        else:
            block = slots_ref[(y - d) & (SPAN - 1)]
            valid = f >= d
        keys[base : base + ROWS, :] = block[0:ROWS]
        values[base : base + ROWS, :] = block[ROWS : 2 * ROWS]
        keys_t[:, base : base + ROWS] = block[0:ROWS].T
        key_seg = block[2 * ROWS :].astype(jnp.float32)[0:1]
        if d == 0:
            query_seg = key_seg
        write_bias(bias, d, key_seg, query_seg, valid)
    for pair in range(4):
        lo_col = pair * 2 * HEAD_DIM
        query_pair = jnp.concatenate(
            [queries[:, lo_col : lo_col + 128], queries[:, lo_col + 128 : lo_col + 256]], axis=0
        )
        grad_pair = jnp.concatenate(
            [grad_ref[:, lo_col : lo_col + 128], grad_ref[:, lo_col + 128 : lo_col + 256]], axis=0
        )
        top = head_scores(keys, bias, scores, query_pair)
        total = jnp.zeros((1, 2 * ROWS), jnp.float32)
        mixed = jnp.zeros((1, 2 * ROWS), jnp.float32)
        for lo in range(0, KEYS, STEP):
            weights = jnp.exp2(scores[lo : lo + STEP, :] - top)
            prob_grad = nt_dot(values[lo : lo + STEP, :], grad_pair)
            total = total + jnp.sum(weights, axis=0, keepdims=True)
            mixed = mixed + jnp.sum(weights * prob_grad, axis=0, keepdims=True)
            scores[lo : lo + STEP, :] = weights
            prob_grads[lo : lo + STEP, :] = prob_grad
        inverse = 1.0 / total
        delta = mixed * inverse
        query_sum = jnp.zeros((HEAD_DIM, 2 * ROWS), jnp.float32)
        for lo in range(0, KEYS, STEP):
            probabilities = scores[lo : lo + STEP, :] * inverse
            score_grad = (probabilities * (prob_grads[lo : lo + STEP, :] - delta)).astype(
                jnp.bfloat16
            )
            value_part = nn_dot(probabilities.astype(jnp.bfloat16), grad_pair)
            key_part = nn_dot(score_grad, query_pair)
            query_sum = query_sum + nn_dot(keys_t[:, lo : lo + STEP], score_grad)
            if pair == 0:
                value_sum[lo : lo + STEP, :] = value_part
                key_sum[lo : lo + STEP, :] = key_part
            else:
                value_sum[lo : lo + STEP, :] += value_part
                key_sum[lo : lo + STEP, :] += key_part
        result = (query_sum * (1.0 / math.sqrt(HEAD_DIM))).T.astype(jnp.bfloat16)
        query_grad_ref[:, lo_col : lo_col + 128] = result[0:128]
        query_grad_ref[:, lo_col + 128 : lo_col + 256] = result[128:256]
    own_part_ref[0:ROWS, :] = key_sum[0:ROWS, :]
    own_part_ref[ROWS : 2 * ROWS, :] = value_sum[0:ROWS, :]
    for d in range(1, HALO):
        key_out = key_sum[d * ROWS : (d + 1) * ROWS, :].astype(jnp.bfloat16)
        value_out = value_sum[d * ROWS : (d + 1) * ROWS, :].astype(jnp.bfloat16)
        if d == HALO - 1:
            send_nine_ref[0:ROWS, :] = key_out
            send_nine_ref[ROWS : 2 * ROWS, :] = value_out
        else:
            slot = (y - d) & (SPAN - 1)
            send_ref[slot, 0:ROWS, :] = key_out
            send_ref[slot, ROWS : 2 * ROWS, :] = value_out


VMEM = pl.BlockSpec(memory_space=pltpu.VMEM)
ANY = pl.BlockSpec(memory_space=pl.ANY)


def wide_ids(ids_ref):
    return jnp.broadcast_to(ids_ref[...].astype(jnp.float32), (16, 128)).astype(jnp.bfloat16)


def prepare_kernel(
    held_key_ref, held_value_ref, held_ids_ref, key_ref, value_ref, ids_ref, cut_ref, forward_ref
):
    held_ids = wide_ids(held_ids_ref)[0:8]
    for t in range(PIECES):
        cut = jnp.concatenate(
            [
                held_key_ref[0, :, t * 128 : (t + 1) * 128],
                held_value_ref[0, :, t * 128 : (t + 1) * 128],
                held_ids,
            ],
            axis=0,
        )
        for copy in range(4):
            cut_ref[copy * PIECES + t] = cut
    forward_ref[0:ROWS, :] = key_ref[0]
    forward_ref[ROWS : 2 * ROWS, :] = value_ref[0]
    forward_ref[2 * ROWS :, :] = wide_ids(ids_ref)


def split_kernel(query_ref, *part_refs):
    t = lax.axis_index("tp").astype(jnp.int32)
    for apart, ref in enumerate(part_refs):
        lo = pl.multiple_of((t ^ apart) * 1024, 1024)
        ref[...] = query_ref[:, pl.ds(lo, 1024)]


def outgoing_kernel(cuts_ref, forward_ref, forward_cross_ref, *refs):
    own_ref, outgoing_ref, stacked_ref = refs[-3:]
    f, y, upper = fsdp_place()
    side = jnp.where(lax.axis_index("section") < 4, 2 * PIECES, 0)
    row = jnp.where(upper, PIECES, 0)

    def whole(first):
        cuts = [cuts_ref[first + piece] for piece in range(PIECES)]
        ids = cuts[0][2 * PIECE :]
        return jnp.concatenate(
            [cut[:PIECE] for cut in cuts] + [cut[PIECE : 2 * PIECE] for cut in cuts] + [ids, ids],
            axis=0,
        )

    own = whole(side + row)
    crossed = whole(side + PIECES - row)
    own_ref[...] = own
    for target in range(SPAN):
        outgoing_ref[target] = jnp.where(upper & (target <= y), crossed, own)
    stacked_ref[0] = forward_ref[...]
    stacked_ref[1] = forward_cross_ref[...]


def reduce_kernel(parts_ref, own_part_ref, *refs):
    same_ref, other_ref = refs[-2:]
    f, y, upper = fsdp_place()
    same = own_part_ref[...]
    other = jnp.zeros((2 * ROWS, HEAD_DIM), jnp.float32)
    for source in range(SPAN):
        part = parts_ref[source].astype(jnp.float32)
        later = source > y
        same = same + jnp.where(later, part, 0.0)
        other = other + jnp.where(later, 0.0, part)
    same_ref[...] = same
    other_ref[...] = other.astype(jnp.bfloat16)


def finish_kernel(same_ref, from_upper_ref, from_nine_ref, key_grad_ref, value_grad_ref):
    f, y, upper = fsdp_place()
    late = from_upper_ref[...].astype(jnp.float32) + from_nine_ref[...].astype(jnp.float32)
    final = same_ref[...] + jnp.where(upper, 0.0, late)
    key_grad_ref[0] = (final[:ROWS] * (1.0 / math.sqrt(HEAD_DIM))).astype(jnp.bfloat16)
    value_grad_ref[0] = final[ROWS:].astype(jnp.bfloat16)


def run_small(kernel, name, limit, shapes, *arrays, waits=(), flops=0):
    return pl.pallas_call(
        kernel,
        out_shape=tuple(
            jax.ShapeDtypeStruct(shape[:-1] if shape[-1] is jnp.float32 else shape, jnp.float32)
            if shape[-1] is jnp.float32
            else jax.ShapeDtypeStruct(shape, jnp.bfloat16)
            for shape in shapes
        ),
        in_specs=[VMEM] * len(arrays) + [ANY] * len(waits),
        out_specs=(VMEM,) * len(shapes),
        compiler_params=pltpu.CompilerParams(vmem_limit_bytes=limit) if limit else None,
        cost_estimate=pl.CostEstimate(flops=int(flops), bytes_accessed=0, transcendentals=0)
        if flops
        else None,
        name=name,
    )(*arrays, *waits)


def run_forward(query, gathered):
    return pl.pallas_call(
        forward_kernel,
        out_shape=(
            jax.ShapeDtypeStruct((ROWS, 1024), jnp.bfloat16),
            jax.ShapeDtypeStruct((8, 128), jnp.float32),
        ),
        in_specs=[VMEM, VMEM],
        out_specs=(VMEM, VMEM),
        scratch_shapes=[
            pltpu.VMEM((KEYS, HEAD_DIM), jnp.bfloat16),
            pltpu.VMEM((HEAD_DIM, KEYS), jnp.bfloat16),
            pltpu.VMEM((KEYS, ROWS), jnp.float32),
            pltpu.VMEM((KEYS, 2 * ROWS), jnp.float32),
        ],
        compiler_params=pltpu.CompilerParams(vmem_limit_bytes=VMEM_LIMIT),
        cost_estimate=pl.CostEstimate(
            flops=2 * 2 * 1024 * KEYS * 128, bytes_accessed=3_000_000, transcendentals=1024 * KEYS
        ),
        name="forward_attention",
    )(query, gathered)


def run_backward(queries, own, slots, nine, grad):
    return pl.pallas_call(
        backward_kernel,
        out_shape=(
            jax.ShapeDtypeStruct((ROWS, 1024), jnp.bfloat16),
            jax.ShapeDtypeStruct((SPAN, 2 * ROWS, HEAD_DIM), jnp.bfloat16),
            jax.ShapeDtypeStruct((2 * ROWS, HEAD_DIM), jnp.bfloat16),
            jax.ShapeDtypeStruct((2 * ROWS, HEAD_DIM), jnp.float32),
        ),
        in_specs=[VMEM] * 8,
        out_specs=(VMEM, VMEM, VMEM, VMEM),
        scratch_shapes=[
            pltpu.VMEM((ROWS, 1024), jnp.bfloat16),
            pltpu.VMEM((KEYS, HEAD_DIM), jnp.bfloat16),
            pltpu.VMEM((HEAD_DIM, KEYS), jnp.bfloat16),
            pltpu.VMEM((KEYS, HEAD_DIM), jnp.bfloat16),
            pltpu.VMEM((KEYS, ROWS), jnp.float32),
            pltpu.VMEM((KEYS, 2 * ROWS), jnp.float32),
            pltpu.VMEM((KEYS, 2 * ROWS), jnp.float32),
            pltpu.VMEM((KEYS, HEAD_DIM), jnp.float32),
            pltpu.VMEM((KEYS, HEAD_DIM), jnp.float32),
        ],
        compiler_params=pltpu.CompilerParams(vmem_limit_bytes=VMEM_LIMIT),
        cost_estimate=pl.CostEstimate(
            flops=1_000_000, bytes_accessed=0, transcendentals=0
        ),
        name="backward_attention",
    )(*queries, own, slots, nine, grad)


def local(
    queries,
    key_rows,
    values,
    segments,
    held_queries,
    held_keys,
    held_values,
    held_segments,
    out_grad,
):
    query_back = lax.ppermute(held_queries[0], "section", SECTION_PAIRS)
    cuts, forward_part = run_small(
        prepare_kernel,
        "prepare",
        None,
        ((4 * PIECES, CUT, 128), (BLOCK, 128)),
        held_keys,
        held_values,
        held_segments,
        key_rows,
        values,
        segments,
    )
    cuts = lax.all_to_all(
        cuts,
        ("section", "fsdp", "tp"),
        split_axis=0,
        concat_axis=0,
        tiled=False,
        axis_index_groups=MIRROR_GROUPS,
    )
    forward_cross = lax.ppermute(forward_part, "fsdp", FSDP_SWAP)
    parts = run_small(
        split_kernel, "split", SMALL_LIMIT, ((PIECE, 1024),) * 4, query_back, flops=3e10
    )
    stash = [parts[0]] + [lax.ppermute(parts[d], "tp", TP_ROUTES[d]) for d in (1, 2, 3)]
    own, outgoing, stacked = run_small(
        outgoing_kernel,
        "outgoing",
        SMALL_LIMIT,
        ((BLOCK, 128), (SPAN, BLOCK, 128), (2, BLOCK, 128)),
        cuts,
        forward_part,
        forward_cross,
        waits=stash[1:2],
    )
    slots = lax.all_to_all(
        outgoing, "fsdp", split_axis=0, concat_axis=0, tiled=False, axis_index_groups=ROW_GROUPS
    )
    nine = lax.ppermute(own, "fsdp", FSDP_NINE)
    gathered = lax.all_gather(
        stacked, "fsdp", axis=0, tiled=True, axis_index_groups=ROW_GROUPS
    )

    query_grad, send, send_nine, own_part = run_backward(stash, own, slots, nine, out_grad[0])
    parts = lax.all_to_all(
        send, "fsdp", split_axis=0, concat_axis=0, tiled=False, axis_index_groups=ROW_GROUPS
    )
    from_nine = lax.ppermute(send_nine, "fsdp", FSDP_NINE)
    attn_out, mark = run_forward(queries[0], gathered)

    same_row, other_row = run_small(
        reduce_kernel,
        "reduce",
        SMALL_LIMIT,
        ((2 * ROWS, 128, jnp.float32), (2 * ROWS, 128)),
        parts,
        own_part,
        waits=(mark,),
    )
    from_upper = lax.ppermute(other_row, "fsdp", FSDP_SWAP)
    key_grad, value_grad = run_small(
        finish_kernel,
        "finish",
        SMALL_LIMIT,
        ((1, ROWS, 128), (1, ROWS, 128)),
        same_row,
        from_upper,
        from_nine,
    )
    return (attn_out[None], query_grad[None], key_grad, value_grad)


def solution(mesh):
    return jax.shard_map(
        local,
        mesh=mesh,
        in_specs=(
            P("section", "fsdp", "tp"),
            P("section", "fsdp", "tp"),
            P("section", "fsdp", "tp"),
            P("section", "fsdp"),
            P("section", ("fsdp", "tp"), None),
            P("section", ("fsdp", "tp"), None),
            P("section", ("fsdp", "tp"), None),
            P("section", "fsdp"),
            P("section", "fsdp", "tp"),
        ),
        out_specs=(
            P("section", "fsdp", "tp"),
            P("section", "fsdp", "tp"),
            P("section", "fsdp", "tp"),
            P("section", "fsdp", "tp"),
        ),
        check_vma=False,
    )
```

```python
import functools
import math

import jax
import jax.numpy as jnp
from jax import lax
from jax.experimental import pallas as pl
from jax.experimental.pallas import tpu as pltpu
from jax.sharding import PartitionSpec as P

HEAD_DIM = 128
ROWS = 128
PIECES = 4
PIECE = ROWS // PIECES
HALO = 10
KEYS = HALO * ROWS
SPAN = 8
HIDDEN = -1e30
TO_LOG2 = math.log2(math.e) / math.sqrt(HEAD_DIM)
STEP = 256
VMEM_LIMIT = 24 * 1024 * 1024
SMALL_LIMIT = 8 * 1024 * 1024

BLOCK = 2 * ROWS + 16
CUT = 2 * PIECE + 8

FSDP_UP = {d: [(f, f + d) for f in range(16 - d)] for d in (1, 2, 4, 6, 8)}
FSDP_SWAP = [(f, f ^ 8) for f in range(16)]
FSDP_NINE = [(f, f + 9) for f in range(7)] + [(f + 9, f) for f in range(7)]
SECTION_PAIRS = [(s, 7 - s) for s in range(8)]
TP_NEAR = [(t, t ^ 1) for t in range(4)]
TP_FAR = [(t, t ^ 2) for t in range(4)]
MIRROR_GROUPS = [
    [(s * 16 + z * 8 + y) * 4 + t for s in (k, 7 - k) for z in range(2) for t in range(4)]
    for k in range(4)
    for y in range(8)
]
ROW_GROUPS = [[z * 8 + y for y in range(8)] for z in range(2)]


def fsdp_place():
    f = lax.axis_index("fsdp").astype(jnp.int32)
    return f, f & (SPAN - 1), f >= SPAN


def nt_dot(a, b):
    return lax.dot_general(a, b, (((1,), (1,)), ((), ())), preferred_element_type=jnp.float32)


def nn_dot(a, b):
    return jnp.dot(a, b, preferred_element_type=jnp.float32)


def write_bias(bias_ref, d, key_seg, query_seg, valid):
    key_wide = jnp.broadcast_to(key_seg, (ROWS, ROWS)).T
    seen = key_wide == jnp.broadcast_to(query_seg, (ROWS, ROWS))
    if d == 0:
        key_pos = lax.broadcasted_iota(jnp.int32, (ROWS, ROWS), 0)
        query_pos = lax.broadcasted_iota(jnp.int32, (ROWS, ROWS), 1)
        seen = seen & (key_pos <= query_pos)
        bias_ref[0:ROWS, :] = jnp.where(seen, 0.0, HIDDEN)
    else:
        shown = jnp.where(valid, 0.0, HIDDEN).astype(jnp.float32)
        bias_ref[d * ROWS : (d + 1) * ROWS, :] = jnp.where(seen, shown, HIDDEN)


def head_scores(keys_ref, bias_ref, scores_ref, query_pair):
    top = jnp.full((1, 2 * ROWS), HIDDEN, jnp.float32)
    for lo in range(0, KEYS, STEP):
        bias = bias_ref[lo : lo + STEP, :]
        raw = nt_dot(keys_ref[lo : lo + STEP, :], query_pair)
        scores = raw * TO_LOG2 + jnp.concatenate([bias, bias], axis=1)
        scores_ref[lo : lo + STEP, :] = scores
        top = jnp.maximum(top, jnp.max(scores, axis=0, keepdims=True))
    return top


def forward_kernel(
    query_ref, pair_0_ref, pair_2_ref, pair_4_ref, pair_6_ref, pair_8_ref, out_ref, mark_ref, keys, values_t, bias, scores
):
    f, y, upper = fsdp_place()
    pairs = (pair_0_ref, pair_2_ref, pair_4_ref, pair_6_ref, pair_8_ref)
    for d in range(HALO):
        valid = f >= d
        block = pairs[d >> 1][1 - (d & 1)]
        keys[d * ROWS : (d + 1) * ROWS, :] = block[0:ROWS]
        values_t[:, d * ROWS : (d + 1) * ROWS] = block[ROWS : 2 * ROWS].T
        key_seg = block[2 * ROWS :].astype(jnp.float32)[0:1]
        if d == 0:
            query_seg = key_seg
        write_bias(bias, d, key_seg, query_seg, valid)
    for pair in range(4):
        lo_col = pair * 2 * HEAD_DIM
        query_pair = jnp.concatenate(
            [query_ref[:, lo_col : lo_col + 128], query_ref[:, lo_col + 128 : lo_col + 256]], axis=0
        )
        top = head_scores(keys, bias, scores, query_pair)
        total = jnp.zeros((1, 2 * ROWS), jnp.float32)
        summed = jnp.zeros((HEAD_DIM, 2 * ROWS), jnp.float32)
        for lo in range(0, KEYS, STEP):
            weights = jnp.exp2(scores[lo : lo + STEP, :] - top)
            total = total + jnp.sum(weights, axis=0, keepdims=True)
            summed = summed + nn_dot(values_t[:, lo : lo + STEP], weights.astype(jnp.bfloat16))
        result = (summed / total).T.astype(jnp.bfloat16)
        out_ref[:, lo_col : lo_col + 128] = result[0:128]
        out_ref[:, lo_col + 128 : lo_col + 256] = result[128:256]
    mark_ref[...] = jnp.zeros((8, 128), jnp.float32)


def backward_kernel(
    kept_ref,
    near_ref,
    far_ref,
    own_ref,
    slots_ref,
    nine_ref,
    grad_ref,
    query_grad_ref,
    send_ref,
    send_nine_ref,
    own_part_ref,
    queries,
    keys,
    keys_t,
    values,
    bias,
    scores,
    prob_grads,
    key_sum,
    value_sum,
):
    f, y, upper = fsdp_place()
    t = lax.axis_index("tp").astype(jnp.int32)
    for apart, piece in enumerate((kept_ref[0], near_ref[0], far_ref[0], far_ref[1])):
        at = pl.multiple_of((t ^ apart) * PIECE, PIECE)
        queries[pl.ds(at, PIECE), :] = piece
    for d in range(HALO):
        base = d * ROWS
        if d == 0:
            block = own_ref[...]
            valid = True
        elif d == HALO - 1:
            block = nine_ref[...]
            valid = upper & (y >= 1)
        else:
            block = slots_ref[(y - d) & (SPAN - 1)]
            valid = f >= d
        keys[base : base + ROWS, :] = block[0:ROWS]
        values[base : base + ROWS, :] = block[ROWS : 2 * ROWS]
        keys_t[:, base : base + ROWS] = block[0:ROWS].T
        key_seg = block[2 * ROWS :].astype(jnp.float32)[0:1]
        if d == 0:
            query_seg = key_seg
        write_bias(bias, d, key_seg, query_seg, valid)
    for pair in range(4):
        lo_col = pair * 2 * HEAD_DIM
        query_pair = jnp.concatenate(
            [queries[:, lo_col : lo_col + 128], queries[:, lo_col + 128 : lo_col + 256]], axis=0
        )
        grad_pair = jnp.concatenate(
            [grad_ref[:, lo_col : lo_col + 128], grad_ref[:, lo_col + 128 : lo_col + 256]], axis=0
        )
        top = head_scores(keys, bias, scores, query_pair)
        total = jnp.zeros((1, 2 * ROWS), jnp.float32)
        mixed = jnp.zeros((1, 2 * ROWS), jnp.float32)
        for lo in range(0, KEYS, STEP):
            weights = jnp.exp2(scores[lo : lo + STEP, :] - top)
            prob_grad = nt_dot(values[lo : lo + STEP, :], grad_pair)
            total = total + jnp.sum(weights, axis=0, keepdims=True)
            mixed = mixed + jnp.sum(weights * prob_grad, axis=0, keepdims=True)
            scores[lo : lo + STEP, :] = weights
            prob_grads[lo : lo + STEP, :] = prob_grad
        inverse = 1.0 / total
        delta = mixed * inverse
        query_sum = jnp.zeros((HEAD_DIM, 2 * ROWS), jnp.float32)
        for lo in range(0, KEYS, STEP):
            probabilities = scores[lo : lo + STEP, :] * inverse
            score_grad = (probabilities * (prob_grads[lo : lo + STEP, :] - delta)).astype(
                jnp.bfloat16
            )
            value_part = nn_dot(probabilities.astype(jnp.bfloat16), grad_pair)
            key_part = nn_dot(score_grad, query_pair)
            query_sum = query_sum + nn_dot(keys_t[:, lo : lo + STEP], score_grad)
            if pair == 0:
                value_sum[lo : lo + STEP, :] = value_part
                key_sum[lo : lo + STEP, :] = key_part
            else:
                value_sum[lo : lo + STEP, :] += value_part
                key_sum[lo : lo + STEP, :] += key_part
        result = (query_sum * (1.0 / math.sqrt(HEAD_DIM))).T.astype(jnp.bfloat16)
        query_grad_ref[:, lo_col : lo_col + 128] = result[0:128]
        query_grad_ref[:, lo_col + 128 : lo_col + 256] = result[128:256]
    own_part_ref[0:ROWS, :] = key_sum[0:ROWS, :]
    own_part_ref[ROWS : 2 * ROWS, :] = value_sum[0:ROWS, :]
    for d in range(1, HALO):
        key_out = key_sum[d * ROWS : (d + 1) * ROWS, :].astype(jnp.bfloat16)
        value_out = value_sum[d * ROWS : (d + 1) * ROWS, :].astype(jnp.bfloat16)
        if d == HALO - 1:
            send_nine_ref[0:ROWS, :] = key_out
            send_nine_ref[ROWS : 2 * ROWS, :] = value_out
        else:
            slot = (y - d) & (SPAN - 1)
            send_ref[slot, 0:ROWS, :] = key_out
            send_ref[slot, ROWS : 2 * ROWS, :] = value_out


VMEM = pl.BlockSpec(memory_space=pltpu.VMEM)
ANY = pl.BlockSpec(memory_space=pl.ANY)


def wide_ids(ids_ref):
    return jnp.broadcast_to(ids_ref[...].astype(jnp.float32), (16, 128)).astype(jnp.bfloat16)


def prepare_kernel(
    held_key_ref, held_value_ref, held_ids_ref, key_ref, value_ref, ids_ref, cut_ref, forward_ref
):
    held_ids = wide_ids(held_ids_ref)[0:8]
    for t in range(PIECES):
        cut = jnp.concatenate(
            [
                held_key_ref[0, :, t * 128 : (t + 1) * 128],
                held_value_ref[0, :, t * 128 : (t + 1) * 128],
                held_ids,
            ],
            axis=0,
        )
        for copy in range(4):
            cut_ref[copy * PIECES + t] = cut
    forward_ref[0:ROWS, :] = key_ref[0]
    forward_ref[ROWS : 2 * ROWS, :] = value_ref[0]
    forward_ref[2 * ROWS :, :] = wide_ids(ids_ref)


def split_kernel(query_ref, kept_ref, near_ref):
    t = lax.axis_index("tp").astype(jnp.int32)
    for apart in range(PIECES):
        lo = pl.multiple_of((t ^ apart) * 1024, 1024)
        ref = near_ref if apart & 1 else kept_ref
        ref[apart >> 1] = query_ref[:, pl.ds(lo, 1024)]


def pass_on_kernel(kept_ref, near_ref, far_ref):
    far_ref[0] = kept_ref[1]
    far_ref[1] = near_ref[1]


def outgoing_kernel(cuts_ref, forward_ref, forward_before_ref, *refs):
    own_ref, outgoing_ref, forward_pair_ref = refs[-3:]
    f, y, upper = fsdp_place()
    side = jnp.where(lax.axis_index("section") < 4, 2 * PIECES, 0)
    row = jnp.where(upper, PIECES, 0)

    def whole(first):
        cuts = [cuts_ref[first + piece] for piece in range(PIECES)]
        ids = cuts[0][2 * PIECE :]
        return jnp.concatenate(
            [cut[:PIECE] for cut in cuts] + [cut[PIECE : 2 * PIECE] for cut in cuts] + [ids, ids],
            axis=0,
        )

    own = whole(side + row)
    crossed = whole(side + PIECES - row)
    own_ref[...] = own
    for target in range(SPAN):
        outgoing_ref[target] = jnp.where(upper & (target <= y), crossed, own)
    forward_pair_ref[0] = forward_before_ref[...]
    forward_pair_ref[1] = forward_ref[...]


def reduce_kernel(parts_ref, own_part_ref, *refs):
    same_ref, other_ref = refs[-2:]
    f, y, upper = fsdp_place()
    same = own_part_ref[...]
    other = jnp.zeros((2 * ROWS, HEAD_DIM), jnp.float32)
    for source in range(SPAN):
        part = parts_ref[source].astype(jnp.float32)
        later = source > y
        same = same + jnp.where(later, part, 0.0)
        other = other + jnp.where(later, 0.0, part)
    same_ref[...] = same
    other_ref[...] = other.astype(jnp.bfloat16)


def finish_kernel(same_ref, from_upper_ref, from_nine_ref, key_grad_ref, value_grad_ref):
    f, y, upper = fsdp_place()
    late = from_upper_ref[...].astype(jnp.float32) + from_nine_ref[...].astype(jnp.float32)
    final = same_ref[...] + jnp.where(upper, 0.0, late)
    key_grad_ref[0] = (final[:ROWS] * (1.0 / math.sqrt(HEAD_DIM))).astype(jnp.bfloat16)
    value_grad_ref[0] = final[ROWS:].astype(jnp.bfloat16)


def run_small(kernel, name, limit, shapes, *arrays, waits=(), flops=0):
    return pl.pallas_call(
        kernel,
        out_shape=tuple(
            jax.ShapeDtypeStruct(shape[:-1] if shape[-1] is jnp.float32 else shape, jnp.float32)
            if shape[-1] is jnp.float32
            else jax.ShapeDtypeStruct(shape, jnp.bfloat16)
            for shape in shapes
        ),
        in_specs=[VMEM] * len(arrays) + [ANY] * len(waits),
        out_specs=(VMEM,) * len(shapes),
        compiler_params=pltpu.CompilerParams(vmem_limit_bytes=limit) if limit else None,
        cost_estimate=pl.CostEstimate(flops=int(flops), bytes_accessed=0, transcendentals=0)
        if flops
        else None,
        name=name,
    )(*arrays, *waits)


def run_forward(query, *pairs):
    return pl.pallas_call(
        forward_kernel,
        out_shape=(
            jax.ShapeDtypeStruct((ROWS, 1024), jnp.bfloat16),
            jax.ShapeDtypeStruct((8, 128), jnp.float32),
        ),
        in_specs=[VMEM] * 6,
        out_specs=(VMEM, VMEM),
        scratch_shapes=[
            pltpu.VMEM((KEYS, HEAD_DIM), jnp.bfloat16),
            pltpu.VMEM((HEAD_DIM, KEYS), jnp.bfloat16),
            pltpu.VMEM((KEYS, ROWS), jnp.float32),
            pltpu.VMEM((KEYS, 2 * ROWS), jnp.float32),
        ],
        compiler_params=pltpu.CompilerParams(vmem_limit_bytes=VMEM_LIMIT),
        cost_estimate=pl.CostEstimate(
            flops=2 * 2 * 1024 * KEYS * 128, bytes_accessed=3_000_000, transcendentals=1024 * KEYS
        ),
        name="forward_attention",
    )(query, *pairs)


def run_backward(queries, own, slots, nine, grad):
    return pl.pallas_call(
        backward_kernel,
        out_shape=(
            jax.ShapeDtypeStruct((ROWS, 1024), jnp.bfloat16),
            jax.ShapeDtypeStruct((SPAN, 2 * ROWS, HEAD_DIM), jnp.bfloat16),
            jax.ShapeDtypeStruct((2 * ROWS, HEAD_DIM), jnp.bfloat16),
            jax.ShapeDtypeStruct((2 * ROWS, HEAD_DIM), jnp.float32),
        ),
        in_specs=[VMEM] * 7,
        out_specs=(VMEM, VMEM, VMEM, VMEM),
        scratch_shapes=[
            pltpu.VMEM((ROWS, 1024), jnp.bfloat16),
            pltpu.VMEM((KEYS, HEAD_DIM), jnp.bfloat16),
            pltpu.VMEM((HEAD_DIM, KEYS), jnp.bfloat16),
            pltpu.VMEM((KEYS, HEAD_DIM), jnp.bfloat16),
            pltpu.VMEM((KEYS, ROWS), jnp.float32),
            pltpu.VMEM((KEYS, 2 * ROWS), jnp.float32),
            pltpu.VMEM((KEYS, 2 * ROWS), jnp.float32),
            pltpu.VMEM((KEYS, HEAD_DIM), jnp.float32),
            pltpu.VMEM((KEYS, HEAD_DIM), jnp.float32),
        ],
        compiler_params=pltpu.CompilerParams(vmem_limit_bytes=VMEM_LIMIT),
        cost_estimate=pl.CostEstimate(
            flops=1_000_000, bytes_accessed=0, transcendentals=0
        ),
        name="backward_attention",
    )(*queries, own, slots, nine, grad)


def local(
    queries,
    key_rows,
    values,
    segments,
    held_queries,
    held_keys,
    held_values,
    held_segments,
    out_grad,
):
    query_back = lax.ppermute(held_queries[0], "section", SECTION_PAIRS)
    cuts, forward_part = run_small(
        prepare_kernel,
        "prepare",
        None,
        ((4 * PIECES, CUT, 128), (BLOCK, 128)),
        held_keys,
        held_values,
        held_segments,
        key_rows,
        values,
        segments,
    )
    cuts = lax.all_to_all(
        cuts,
        ("section", "fsdp", "tp"),
        split_axis=0,
        concat_axis=0,
        tiled=False,
        axis_index_groups=MIRROR_GROUPS,
    )
    forward_before = lax.ppermute(forward_part, "fsdp", FSDP_UP[1])
    kept, near = run_small(
        split_kernel, "split", SMALL_LIMIT, ((2, PIECE, 1024),) * 2, query_back, flops=3e10
    )
    near = lax.ppermute(near, "tp", TP_NEAR)
    own, outgoing, forward_pair = run_small(
        outgoing_kernel,
        "outgoing",
        SMALL_LIMIT,
        ((BLOCK, 128), (SPAN, BLOCK, 128), (2, BLOCK, 128)),
        cuts,
        forward_part,
        forward_before,
    )
    slots = lax.all_to_all(
        outgoing, "fsdp", split_axis=0, concat_axis=0, tiled=False, axis_index_groups=ROW_GROUPS
    )
    (far,) = run_small(
        pass_on_kernel, "pass_on", SMALL_LIMIT, ((2, PIECE, 1024),), kept, near, flops=3e10
    )
    far = lax.ppermute(far, "tp", TP_FAR)
    nine = lax.ppermute(own, "fsdp", FSDP_NINE)
    pairs = {d: lax.ppermute(forward_pair, "fsdp", FSDP_UP[d]) for d in (8, 6, 4, 2)}

    query_grad, send, send_nine, own_part = run_backward((kept, near, far), own, slots, nine, out_grad[0])
    parts = lax.all_to_all(
        send, "fsdp", split_axis=0, concat_axis=0, tiled=False, axis_index_groups=ROW_GROUPS
    )
    from_nine = lax.ppermute(send_nine, "fsdp", FSDP_NINE)
    attn_out, mark = run_forward(queries[0], forward_pair, pairs[2], pairs[4], pairs[6], pairs[8])

    same_row, other_row = run_small(
        reduce_kernel,
        "reduce",
        SMALL_LIMIT,
        ((2 * ROWS, 128, jnp.float32), (2 * ROWS, 128)),
        parts,
        own_part,
        waits=(),
    )
    from_upper = lax.ppermute(other_row, "fsdp", FSDP_SWAP)
    key_grad, value_grad = run_small(
        finish_kernel,
        "finish",
        SMALL_LIMIT,
        ((1, ROWS, 128), (1, ROWS, 128)),
        same_row,
        from_upper,
        from_nine,
    )
    return (attn_out[None], query_grad[None], key_grad, value_grad)


def solution(mesh):
    return jax.shard_map(
        local,
        mesh=mesh,
        in_specs=(
            P("section", "fsdp", "tp"),
            P("section", "fsdp", "tp"),
            P("section", "fsdp", "tp"),
            P("section", "fsdp"),
            P("section", ("fsdp", "tp"), None),
            P("section", ("fsdp", "tp"), None),
            P("section", ("fsdp", "tp"), None),
            P("section", "fsdp"),
            P("section", "fsdp", "tp"),
        ),
        out_specs=(
            P("section", "fsdp", "tp"),
            P("section", "fsdp", "tp"),
            P("section", "fsdp", "tp"),
            P("section", "fsdp", "tp"),
        ),
        check_vma=False,
    )
```

```python
import functools
import math

import jax
import jax.numpy as jnp
from jax import lax
from jax.experimental import pallas as pl
from jax.experimental.pallas import tpu as pltpu
from jax.sharding import PartitionSpec as P

HEAD_DIM = 128
ROWS = 128
PIECES = 4
PIECE = ROWS // PIECES
HALO = 10
KEYS = HALO * ROWS
SPAN = 8
HIDDEN = -1e30
TO_LOG2 = math.log2(math.e) / math.sqrt(HEAD_DIM)
STEP = 256
VMEM_LIMIT = 24 * 1024 * 1024
SMALL_LIMIT = 8 * 1024 * 1024

BLOCK = 2 * ROWS + 16
CUT = 2 * PIECE + 8

FSDP_UP = {d: [(f, f + d) for f in range(16 - d)] for d in (1, 2, 4, 6, 8)}
FSDP_SWAP = [(f, f ^ 8) for f in range(16)]
FSDP_NINE = [(f, f + 9) for f in range(7)] + [(f + 9, f) for f in range(7)]
SECTION_PAIRS = [(s, 7 - s) for s in range(8)]
TP_NEAR = [(t, t ^ 1) for t in range(4)]
TP_FAR = [(t, t ^ 2) for t in range(4)]
MIRROR_GROUPS = [
    [(s * 16 + z * 8 + y) * 4 + t for s in (k, 7 - k) for z in range(2) for t in range(4)]
    for k in range(4)
    for y in range(8)
]
ROW_GROUPS = [[z * 8 + y for y in range(8)] for z in range(2)]


def fsdp_place():
    f = lax.axis_index("fsdp").astype(jnp.int32)
    return f, f & (SPAN - 1), f >= SPAN


def nt_dot(a, b):
    return lax.dot_general(a, b, (((1,), (1,)), ((), ())), preferred_element_type=jnp.float32)


def nn_dot(a, b):
    return jnp.dot(a, b, preferred_element_type=jnp.float32)


def write_bias(bias_ref, d, key_seg, query_seg, valid):
    key_wide = jnp.broadcast_to(key_seg, (ROWS, ROWS)).T
    seen = key_wide == jnp.broadcast_to(query_seg, (ROWS, ROWS))
    if d == 0:
        key_pos = lax.broadcasted_iota(jnp.int32, (ROWS, ROWS), 0)
        query_pos = lax.broadcasted_iota(jnp.int32, (ROWS, ROWS), 1)
        seen = seen & (key_pos <= query_pos)
        bias_ref[0:ROWS, :] = jnp.where(seen, 0.0, HIDDEN)
    else:
        shown = jnp.where(valid, 0.0, HIDDEN).astype(jnp.float32)
        bias_ref[d * ROWS : (d + 1) * ROWS, :] = jnp.where(seen, shown, HIDDEN)


def head_scores(keys_ref, bias_ref, scores_ref, query_pair):
    top = jnp.full((1, 2 * ROWS), HIDDEN, jnp.float32)
    for lo in range(0, KEYS, STEP):
        bias = bias_ref[lo : lo + STEP, :]
        raw = nt_dot(keys_ref[lo : lo + STEP, :], query_pair)
        scores = raw * TO_LOG2 + jnp.concatenate([bias, bias], axis=1)
        scores_ref[lo : lo + STEP, :] = scores
        top = jnp.maximum(top, jnp.max(scores, axis=0, keepdims=True))
    return top


def forward_kernel(
    query_ref, pair_0_ref, pair_2_ref, pair_4_ref, pair_6_ref, pair_8_ref, out_ref, mark_ref, keys, values_t, bias, scores
):
    f, y, upper = fsdp_place()
    pairs = (pair_0_ref, pair_2_ref, pair_4_ref, pair_6_ref, pair_8_ref)
    for d in range(HALO):
        valid = f >= d
        block = pairs[d >> 1][1 - (d & 1)]
        keys[d * ROWS : (d + 1) * ROWS, :] = block[0:ROWS]
        values_t[:, d * ROWS : (d + 1) * ROWS] = block[ROWS : 2 * ROWS].T
        key_seg = block[2 * ROWS :].astype(jnp.float32)[0:1]
        if d == 0:
            query_seg = key_seg
        write_bias(bias, d, key_seg, query_seg, valid)
    for pair in range(4):
        lo_col = pair * 2 * HEAD_DIM
        query_pair = jnp.concatenate(
            [query_ref[:, lo_col : lo_col + 128], query_ref[:, lo_col + 128 : lo_col + 256]], axis=0
        )
        top = head_scores(keys, bias, scores, query_pair)
        total = jnp.zeros((1, 2 * ROWS), jnp.float32)
        summed = jnp.zeros((HEAD_DIM, 2 * ROWS), jnp.float32)
        for lo in range(0, KEYS, STEP):
            weights = jnp.exp2(scores[lo : lo + STEP, :] - top)
            total = total + jnp.sum(weights, axis=0, keepdims=True)
            summed = summed + nn_dot(values_t[:, lo : lo + STEP], weights.astype(jnp.bfloat16))
        result = (summed / total).T.astype(jnp.bfloat16)
        out_ref[:, lo_col : lo_col + 128] = result[0:128]
        out_ref[:, lo_col + 128 : lo_col + 256] = result[128:256]
    mark_ref[...] = jnp.zeros((8, 128), jnp.float32)


def backward_kernel(
    kept_ref,
    near_ref,
    far_ref,
    own_ref,
    slots_ref,
    nine_ref,
    grad_ref,
    *refs,
):
    (
        query_grad_ref,
        send_ref,
        send_nine_ref,
        own_part_ref,
        queries,
        keys,
        keys_t,
        values,
        bias,
        scores,
        prob_grads,
        key_sum,
        value_sum,
    ) = refs[1:]
    f, y, upper = fsdp_place()
    t = lax.axis_index("tp").astype(jnp.int32)
    for apart, piece in enumerate((kept_ref[0], near_ref[0], far_ref[0], far_ref[1])):
        at = pl.multiple_of((t ^ apart) * PIECE, PIECE)
        queries[pl.ds(at, PIECE), :] = piece
    for d in range(HALO):
        base = d * ROWS
        if d == 0:
            block = own_ref[...]
            valid = True
        elif d == HALO - 1:
            block = nine_ref[...]
            valid = upper & (y >= 1)
        else:
            block = slots_ref[(y - d) & (SPAN - 1)]
            valid = f >= d
        keys[base : base + ROWS, :] = block[0:ROWS]
        values[base : base + ROWS, :] = block[ROWS : 2 * ROWS]
        keys_t[:, base : base + ROWS] = block[0:ROWS].T
        key_seg = block[2 * ROWS :].astype(jnp.float32)[0:1]
        if d == 0:
            query_seg = key_seg
        write_bias(bias, d, key_seg, query_seg, valid)
    for pair in range(4):
        lo_col = pair * 2 * HEAD_DIM
        query_pair = jnp.concatenate(
            [queries[:, lo_col : lo_col + 128], queries[:, lo_col + 128 : lo_col + 256]], axis=0
        )
        grad_pair = jnp.concatenate(
            [grad_ref[:, lo_col : lo_col + 128], grad_ref[:, lo_col + 128 : lo_col + 256]], axis=0
        )
        top = head_scores(keys, bias, scores, query_pair)
        total = jnp.zeros((1, 2 * ROWS), jnp.float32)
        mixed = jnp.zeros((1, 2 * ROWS), jnp.float32)
        for lo in range(0, KEYS, STEP):
            weights = jnp.exp2(scores[lo : lo + STEP, :] - top)
            prob_grad = nt_dot(values[lo : lo + STEP, :], grad_pair)
            total = total + jnp.sum(weights, axis=0, keepdims=True)
            mixed = mixed + jnp.sum(weights * prob_grad, axis=0, keepdims=True)
            scores[lo : lo + STEP, :] = weights
            prob_grads[lo : lo + STEP, :] = prob_grad
        inverse = 1.0 / total
        delta = mixed * inverse
        query_sum = jnp.zeros((HEAD_DIM, 2 * ROWS), jnp.float32)
        for lo in range(0, KEYS, STEP):
            probabilities = scores[lo : lo + STEP, :] * inverse
            score_grad = (probabilities * (prob_grads[lo : lo + STEP, :] - delta)).astype(
                jnp.bfloat16
            )
            value_part = nn_dot(probabilities.astype(jnp.bfloat16), grad_pair)
            key_part = nn_dot(score_grad, query_pair)
            query_sum = query_sum + nn_dot(keys_t[:, lo : lo + STEP], score_grad)
            if pair == 0:
                value_sum[lo : lo + STEP, :] = value_part
                key_sum[lo : lo + STEP, :] = key_part
            else:
                value_sum[lo : lo + STEP, :] += value_part
                key_sum[lo : lo + STEP, :] += key_part
        result = (query_sum * (1.0 / math.sqrt(HEAD_DIM))).T.astype(jnp.bfloat16)
        query_grad_ref[:, lo_col : lo_col + 128] = result[0:128]
        query_grad_ref[:, lo_col + 128 : lo_col + 256] = result[128:256]
    own_part_ref[0:ROWS, :] = key_sum[0:ROWS, :]
    own_part_ref[ROWS : 2 * ROWS, :] = value_sum[0:ROWS, :]
    for d in range(1, HALO):
        key_out = key_sum[d * ROWS : (d + 1) * ROWS, :].astype(jnp.bfloat16)
        value_out = value_sum[d * ROWS : (d + 1) * ROWS, :].astype(jnp.bfloat16)
        if d == HALO - 1:
            send_nine_ref[0:ROWS, :] = key_out
            send_nine_ref[ROWS : 2 * ROWS, :] = value_out
        else:
            slot = (y - d) & (SPAN - 1)
            send_ref[slot, 0:ROWS, :] = key_out
            send_ref[slot, ROWS : 2 * ROWS, :] = value_out


VMEM = pl.BlockSpec(memory_space=pltpu.VMEM)
ANY = pl.BlockSpec(memory_space=pl.ANY)


def wide_ids(ids_ref):
    return jnp.broadcast_to(ids_ref[...].astype(jnp.float32), (16, 128)).astype(jnp.bfloat16)


def prepare_kernel(
    held_key_ref, held_value_ref, held_ids_ref, key_ref, value_ref, ids_ref, cut_ref, forward_ref
):
    held_ids = wide_ids(held_ids_ref)[0:8]
    for t in range(PIECES):
        cut = jnp.concatenate(
            [
                held_key_ref[0, :, t * 128 : (t + 1) * 128],
                held_value_ref[0, :, t * 128 : (t + 1) * 128],
                held_ids,
            ],
            axis=0,
        )
        for copy in range(4):
            cut_ref[copy * PIECES + t] = cut
    forward_ref[0:ROWS, :] = key_ref[0]
    forward_ref[ROWS : 2 * ROWS, :] = value_ref[0]
    forward_ref[2 * ROWS :, :] = wide_ids(ids_ref)


def split_kernel(query_ref, kept_ref, near_ref):
    t = lax.axis_index("tp").astype(jnp.int32)
    for apart in range(PIECES):
        lo = pl.multiple_of((t ^ apart) * 1024, 1024)
        ref = near_ref if apart & 1 else kept_ref
        ref[apart >> 1] = query_ref[:, pl.ds(lo, 1024)]


def pass_on_kernel(kept_ref, near_ref, forward_ref, forward_before_ref, far_ref, forward_pair_ref):
    far_ref[0] = kept_ref[1]
    far_ref[1] = near_ref[1]
    forward_pair_ref[0] = forward_before_ref[...]
    forward_pair_ref[1] = forward_ref[...]


def outgoing_kernel(cuts_ref, own_ref, outgoing_ref):
    f, y, upper = fsdp_place()
    side = jnp.where(lax.axis_index("section") < 4, 2 * PIECES, 0)
    row = jnp.where(upper, PIECES, 0)

    def whole(first):
        cuts = [cuts_ref[first + piece] for piece in range(PIECES)]
        ids = cuts[0][2 * PIECE :]
        return jnp.concatenate(
            [cut[:PIECE] for cut in cuts] + [cut[PIECE : 2 * PIECE] for cut in cuts] + [ids, ids],
            axis=0,
        )

    own = whole(side + row)
    crossed = whole(side + PIECES - row)
    own_ref[...] = own
    for target in range(SPAN):
        outgoing_ref[target] = jnp.where(upper & (target <= y), crossed, own)


def reduce_kernel(parts_ref, own_part_ref, *refs):
    same_ref, other_ref = refs[-2:]
    f, y, upper = fsdp_place()
    same = own_part_ref[...]
    other = jnp.zeros((2 * ROWS, HEAD_DIM), jnp.float32)
    for source in range(SPAN):
        part = parts_ref[source].astype(jnp.float32)
        later = source > y
        same = same + jnp.where(later, part, 0.0)
        other = other + jnp.where(later, 0.0, part)
    same_ref[...] = same
    other_ref[...] = other.astype(jnp.bfloat16)


def finish_kernel(same_ref, from_upper_ref, from_nine_ref, key_grad_ref, value_grad_ref):
    f, y, upper = fsdp_place()
    late = from_upper_ref[...].astype(jnp.float32) + from_nine_ref[...].astype(jnp.float32)
    final = same_ref[...] + jnp.where(upper, 0.0, late)
    key_grad_ref[0] = (final[:ROWS] * (1.0 / math.sqrt(HEAD_DIM))).astype(jnp.bfloat16)
    value_grad_ref[0] = final[ROWS:].astype(jnp.bfloat16)


def run_small(kernel, name, limit, shapes, *arrays, waits=(), flops=0):
    return pl.pallas_call(
        kernel,
        out_shape=tuple(
            jax.ShapeDtypeStruct(shape[:-1] if shape[-1] is jnp.float32 else shape, jnp.float32)
            if shape[-1] is jnp.float32
            else jax.ShapeDtypeStruct(shape, jnp.bfloat16)
            for shape in shapes
        ),
        in_specs=[VMEM] * len(arrays) + [ANY] * len(waits),
        out_specs=(VMEM,) * len(shapes),
        compiler_params=pltpu.CompilerParams(vmem_limit_bytes=limit) if limit else None,
        cost_estimate=pl.CostEstimate(flops=int(flops), bytes_accessed=0, transcendentals=0)
        if flops
        else None,
        name=name,
    )(*arrays, *waits)


def run_forward(query, *pairs):
    return pl.pallas_call(
        forward_kernel,
        out_shape=(
            jax.ShapeDtypeStruct((ROWS, 1024), jnp.bfloat16),
            jax.ShapeDtypeStruct((8, 128), jnp.float32),
        ),
        in_specs=[VMEM] * 6,
        out_specs=(VMEM, VMEM),
        scratch_shapes=[
            pltpu.VMEM((KEYS, HEAD_DIM), jnp.bfloat16),
            pltpu.VMEM((HEAD_DIM, KEYS), jnp.bfloat16),
            pltpu.VMEM((KEYS, ROWS), jnp.float32),
            pltpu.VMEM((KEYS, 2 * ROWS), jnp.float32),
        ],
        compiler_params=pltpu.CompilerParams(vmem_limit_bytes=VMEM_LIMIT),
        cost_estimate=pl.CostEstimate(
            flops=2 * 2 * 1024 * KEYS * 128, bytes_accessed=3_000_000, transcendentals=1024 * KEYS
        ),
        name="forward_attention",
    )(query, *pairs)


def run_backward(queries, own, slots, nine, grad, *waits):
    return pl.pallas_call(
        backward_kernel,
        out_shape=(
            jax.ShapeDtypeStruct((ROWS, 1024), jnp.bfloat16),
            jax.ShapeDtypeStruct((SPAN, 2 * ROWS, HEAD_DIM), jnp.bfloat16),
            jax.ShapeDtypeStruct((2 * ROWS, HEAD_DIM), jnp.bfloat16),
            jax.ShapeDtypeStruct((2 * ROWS, HEAD_DIM), jnp.float32),
        ),
        in_specs=[VMEM] * 7 + [ANY] * len(waits),
        out_specs=(VMEM, VMEM, VMEM, VMEM),
        scratch_shapes=[
            pltpu.VMEM((ROWS, 1024), jnp.bfloat16),
            pltpu.VMEM((KEYS, HEAD_DIM), jnp.bfloat16),
            pltpu.VMEM((HEAD_DIM, KEYS), jnp.bfloat16),
            pltpu.VMEM((KEYS, HEAD_DIM), jnp.bfloat16),
            pltpu.VMEM((KEYS, ROWS), jnp.float32),
            pltpu.VMEM((KEYS, 2 * ROWS), jnp.float32),
            pltpu.VMEM((KEYS, 2 * ROWS), jnp.float32),
            pltpu.VMEM((KEYS, HEAD_DIM), jnp.float32),
            pltpu.VMEM((KEYS, HEAD_DIM), jnp.float32),
        ],
        compiler_params=pltpu.CompilerParams(vmem_limit_bytes=VMEM_LIMIT),
        cost_estimate=pl.CostEstimate(
            flops=1_000_000, bytes_accessed=0, transcendentals=0
        ),
        name="backward_attention",
    )(*queries, own, slots, nine, grad, *waits)


def local(
    queries,
    key_rows,
    values,
    segments,
    held_queries,
    held_keys,
    held_values,
    held_segments,
    out_grad,
):
    query_back = lax.ppermute(held_queries[0], "section", SECTION_PAIRS)
    cuts, forward_part = run_small(
        prepare_kernel,
        "prepare",
        None,
        ((4 * PIECES, CUT, 128), (BLOCK, 128)),
        held_keys,
        held_values,
        held_segments,
        key_rows,
        values,
        segments,
    )
    cuts = lax.all_to_all(
        cuts,
        ("section", "fsdp", "tp"),
        split_axis=0,
        concat_axis=0,
        tiled=False,
        axis_index_groups=MIRROR_GROUPS,
    )
    forward_before = lax.ppermute(forward_part, "fsdp", FSDP_UP[1])
    kept, near = run_small(
        split_kernel, "split", SMALL_LIMIT, ((2, PIECE, 1024),) * 2, query_back, flops=3e10
    )
    near = lax.ppermute(near, "tp", TP_NEAR)
    own, outgoing = run_small(
        outgoing_kernel,
        "outgoing",
        SMALL_LIMIT,
        ((BLOCK, 128), (SPAN, BLOCK, 128)),
        cuts,
    )
    slots = lax.all_to_all(
        outgoing, "fsdp", split_axis=0, concat_axis=0, tiled=False, axis_index_groups=ROW_GROUPS
    )
    far, forward_pair = run_small(
        pass_on_kernel,
        "pass_on",
        SMALL_LIMIT,
        ((2, PIECE, 1024), (2, BLOCK, 128)),
        kept,
        near,
        forward_part,
        forward_before,
        flops=3e10,
    )
    far = lax.ppermute(far, "tp", TP_FAR)
    nine = lax.ppermute(own, "fsdp", FSDP_NINE)
    pairs = {d: lax.ppermute(forward_pair, "fsdp", FSDP_UP[d]) for d in (8, 6, 4, 2)}

    query_grad, send, send_nine, own_part = run_backward(
        (kept, near, far), own, slots, nine, out_grad[0], pairs[4]
    )
    parts = lax.all_to_all(
        send, "fsdp", split_axis=0, concat_axis=0, tiled=False, axis_index_groups=ROW_GROUPS
    )
    from_nine = lax.ppermute(send_nine, "fsdp", FSDP_NINE)
    attn_out, mark = run_forward(queries[0], forward_pair, pairs[2], pairs[4], pairs[6], pairs[8])

    same_row, other_row = run_small(
        reduce_kernel,
        "reduce",
        SMALL_LIMIT,
        ((2 * ROWS, 128, jnp.float32), (2 * ROWS, 128)),
        parts,
        own_part,
        waits=(),
    )
    from_upper = lax.ppermute(other_row, "fsdp", FSDP_SWAP)
    key_grad, value_grad = run_small(
        finish_kernel,
        "finish",
        SMALL_LIMIT,
        ((1, ROWS, 128), (1, ROWS, 128)),
        same_row,
        from_upper,
        from_nine,
    )
    return (attn_out[None], query_grad[None], key_grad, value_grad)


def solution(mesh):
    return jax.shard_map(
        local,
        mesh=mesh,
        in_specs=(
            P("section", "fsdp", "tp"),
            P("section", "fsdp", "tp"),
            P("section", "fsdp", "tp"),
            P("section", "fsdp"),
            P("section", ("fsdp", "tp"), None),
            P("section", ("fsdp", "tp"), None),
            P("section", ("fsdp", "tp"), None),
            P("section", "fsdp"),
            P("section", "fsdp", "tp"),
        ),
        out_specs=(
            P("section", "fsdp", "tp"),
            P("section", "fsdp", "tp"),
            P("section", "fsdp", "tp"),
            P("section", "fsdp", "tp"),
        ),
        check_vma=False,
    )
```

```python
import functools
import math

import jax
import jax.numpy as jnp
from jax import lax
from jax.experimental import pallas as pl
from jax.experimental.pallas import tpu as pltpu
from jax.sharding import PartitionSpec as P

HEAD_DIM = 128
ROWS = 128
PIECES = 4
PIECE = ROWS // PIECES
HALO = 10
KEYS = HALO * ROWS
SPAN = 8
HIDDEN = -1e30
TO_LOG2 = math.log2(math.e) / math.sqrt(HEAD_DIM)
STEP = 256
VMEM_LIMIT = 24 * 1024 * 1024
SMALL_LIMIT = 8 * 1024 * 1024

BLOCK = 2 * ROWS + 8
CUT = 2 * PIECE + 8

FSDP_UP = {d: [(f, f + d) for f in range(16 - d)] for d in (1, 2, 4, 6, 8)}
FSDP_SWAP = [(f, f ^ 8) for f in range(16)]
FSDP_NINE = [(f, f + 9) for f in range(7)] + [(f + 9, f) for f in range(7)]
SECTION_PAIRS = [(s, 7 - s) for s in range(8)]
TP_NEAR = [(t, t ^ 1) for t in range(4)]
TP_FAR = [(t, t ^ 2) for t in range(4)]
MIRROR_GROUPS = [
    [(s * 16 + z * 8 + y) * 4 + t for s in (k, 7 - k) for z in range(2) for t in range(4)]
    for k in range(4)
    for y in range(8)
]
ROW_GROUPS = [[z * 8 + y for y in range(8)] for z in range(2)]


def fsdp_place():
    f = lax.axis_index("fsdp").astype(jnp.int32)
    return f, f & (SPAN - 1), f >= SPAN


def nt_dot(a, b):
    return lax.dot_general(a, b, (((1,), (1,)), ((), ())), preferred_element_type=jnp.float32)


def nn_dot(a, b):
    return jnp.dot(a, b, preferred_element_type=jnp.float32)


def write_bias(bias_ref, d, key_seg, query_seg, valid):
    key_wide = jnp.broadcast_to(key_seg, (ROWS, ROWS)).T
    seen = key_wide == jnp.broadcast_to(query_seg, (ROWS, ROWS))
    if d == 0:
        key_pos = lax.broadcasted_iota(jnp.int32, (ROWS, ROWS), 0)
        query_pos = lax.broadcasted_iota(jnp.int32, (ROWS, ROWS), 1)
        seen = seen & (key_pos <= query_pos)
        bias_ref[0:ROWS, :] = jnp.where(seen, 0.0, HIDDEN)
    else:
        shown = jnp.where(valid, 0.0, HIDDEN).astype(jnp.float32)
        bias_ref[d * ROWS : (d + 1) * ROWS, :] = jnp.where(seen, shown, HIDDEN)


def head_scores(keys_ref, bias_ref, scores_ref, query_pair):
    top = jnp.full((1, 2 * ROWS), HIDDEN, jnp.float32)
    for lo in range(0, KEYS, STEP):
        bias = bias_ref[lo : lo + STEP, :]
        raw = nt_dot(keys_ref[lo : lo + STEP, :], query_pair)
        scores = raw * TO_LOG2 + jnp.concatenate([bias, bias], axis=1)
        scores_ref[lo : lo + STEP, :] = scores
        top = jnp.maximum(top, jnp.max(scores, axis=0, keepdims=True))
    return top


def forward_kernel(
    query_ref, pair_0_ref, pair_2_ref, pair_4_ref, pair_6_ref, pair_8_ref, out_ref, mark_ref, keys, values_t, bias, scores
):
    f, y, upper = fsdp_place()
    pairs = (pair_0_ref, pair_2_ref, pair_4_ref, pair_6_ref, pair_8_ref)
    for d in range(HALO):
        valid = f >= d
        block = pairs[d >> 1][1 - (d & 1)]
        keys[d * ROWS : (d + 1) * ROWS, :] = block[0:ROWS]
        values_t[:, d * ROWS : (d + 1) * ROWS] = block[ROWS : 2 * ROWS].T
        key_seg = block[2 * ROWS :].astype(jnp.float32)[0:1]
        if d == 0:
            query_seg = key_seg
        write_bias(bias, d, key_seg, query_seg, valid)
    for pair in range(4):
        lo_col = pair * 2 * HEAD_DIM
        query_pair = jnp.concatenate(
            [query_ref[:, lo_col : lo_col + 128], query_ref[:, lo_col + 128 : lo_col + 256]], axis=0
        )
        top = head_scores(keys, bias, scores, query_pair)
        total = jnp.zeros((1, 2 * ROWS), jnp.float32)
        summed = jnp.zeros((HEAD_DIM, 2 * ROWS), jnp.float32)
        for lo in range(0, KEYS, STEP):
            weights = jnp.exp2(scores[lo : lo + STEP, :] - top)
            total = total + jnp.sum(weights, axis=0, keepdims=True)
            summed = summed + nn_dot(values_t[:, lo : lo + STEP], weights.astype(jnp.bfloat16))
        result = (summed / total).T.astype(jnp.bfloat16)
        out_ref[:, lo_col : lo_col + 128] = result[0:128]
        out_ref[:, lo_col + 128 : lo_col + 256] = result[128:256]
    mark_ref[...] = jnp.zeros((8, 128), jnp.float32)


def backward_kernel(
    kept_ref,
    near_ref,
    far_ref,
    own_ref,
    slots_ref,
    nine_ref,
    grad_ref,
    *refs,
):
    (
        query_grad_ref,
        send_ref,
        send_nine_ref,
        own_part_ref,
        queries,
        keys,
        keys_t,
        values,
        bias,
        scores,
        prob_grads,
        key_sum,
        value_sum,
    ) = refs[1:]
    f, y, upper = fsdp_place()
    t = lax.axis_index("tp").astype(jnp.int32)
    for apart, piece in enumerate((kept_ref[0], near_ref[0], far_ref[0], far_ref[1])):
        at = pl.multiple_of((t ^ apart) * PIECE, PIECE)
        queries[pl.ds(at, PIECE), :] = piece
    for d in range(HALO):
        base = d * ROWS
        if d == 0:
            block = own_ref[...]
            valid = True
        elif d == HALO - 1:
            block = nine_ref[...]
            valid = upper & (y >= 1)
        else:
            block = slots_ref[(y - d) & (SPAN - 1)]
            valid = f >= d
        keys[base : base + ROWS, :] = block[0:ROWS]
        values[base : base + ROWS, :] = block[ROWS : 2 * ROWS]
        keys_t[:, base : base + ROWS] = block[0:ROWS].T
        key_seg = block[2 * ROWS :].astype(jnp.float32)[0:1]
        if d == 0:
            query_seg = key_seg
        write_bias(bias, d, key_seg, query_seg, valid)
    for pair in range(4):
        lo_col = pair * 2 * HEAD_DIM
        query_pair = jnp.concatenate(
            [queries[:, lo_col : lo_col + 128], queries[:, lo_col + 128 : lo_col + 256]], axis=0
        )
        grad_pair = jnp.concatenate(
            [grad_ref[:, lo_col : lo_col + 128], grad_ref[:, lo_col + 128 : lo_col + 256]], axis=0
        )
        top = head_scores(keys, bias, scores, query_pair)
        total = jnp.zeros((1, 2 * ROWS), jnp.float32)
        mixed = jnp.zeros((1, 2 * ROWS), jnp.float32)
        for lo in range(0, KEYS, STEP):
            weights = jnp.exp2(scores[lo : lo + STEP, :] - top)
            prob_grad = nt_dot(values[lo : lo + STEP, :], grad_pair)
            total = total + jnp.sum(weights, axis=0, keepdims=True)
            mixed = mixed + jnp.sum(weights * prob_grad, axis=0, keepdims=True)
            scores[lo : lo + STEP, :] = weights
            prob_grads[lo : lo + STEP, :] = prob_grad
        inverse = 1.0 / total
        delta = mixed * inverse
        query_sum = jnp.zeros((HEAD_DIM, 2 * ROWS), jnp.float32)
        for lo in range(0, KEYS, STEP):
            probabilities = scores[lo : lo + STEP, :] * inverse
            score_grad = (probabilities * (prob_grads[lo : lo + STEP, :] - delta)).astype(
                jnp.bfloat16
            )
            value_part = nn_dot(probabilities.astype(jnp.bfloat16), grad_pair)
            key_part = nn_dot(score_grad, query_pair)
            query_sum = query_sum + nn_dot(keys_t[:, lo : lo + STEP], score_grad)
            if pair == 0:
                value_sum[lo : lo + STEP, :] = value_part
                key_sum[lo : lo + STEP, :] = key_part
            else:
                value_sum[lo : lo + STEP, :] += value_part
                key_sum[lo : lo + STEP, :] += key_part
        result = (query_sum * (1.0 / math.sqrt(HEAD_DIM))).T.astype(jnp.bfloat16)
        query_grad_ref[:, lo_col : lo_col + 128] = result[0:128]
        query_grad_ref[:, lo_col + 128 : lo_col + 256] = result[128:256]
    own_part_ref[0:ROWS, :] = key_sum[0:ROWS, :]
    own_part_ref[ROWS : 2 * ROWS, :] = value_sum[0:ROWS, :]
    for d in range(1, HALO):
        key_out = key_sum[d * ROWS : (d + 1) * ROWS, :].astype(jnp.bfloat16)
        value_out = value_sum[d * ROWS : (d + 1) * ROWS, :].astype(jnp.bfloat16)
        if d == HALO - 1:
            send_nine_ref[0:ROWS, :] = key_out
            send_nine_ref[ROWS : 2 * ROWS, :] = value_out
        else:
            slot = (y - d) & (SPAN - 1)
            send_ref[slot, 0:ROWS, :] = key_out
            send_ref[slot, ROWS : 2 * ROWS, :] = value_out


VMEM = pl.BlockSpec(memory_space=pltpu.VMEM)
ANY = pl.BlockSpec(memory_space=pl.ANY)


def wide_ids(ids_ref):
    return jnp.broadcast_to(ids_ref[...].astype(jnp.float32), (8, 128)).astype(jnp.bfloat16)


def prepare_kernel(
    held_key_ref, held_value_ref, held_ids_ref, key_ref, value_ref, ids_ref, cut_ref, forward_ref
):
    held_ids = wide_ids(held_ids_ref)
    for t in range(PIECES):
        cut = jnp.concatenate(
            [
                held_key_ref[0, :, t * 128 : (t + 1) * 128],
                held_value_ref[0, :, t * 128 : (t + 1) * 128],
                held_ids,
            ],
            axis=0,
        )
        for copy in range(4):
            cut_ref[copy * PIECES + t] = cut
    forward_ref[0:ROWS, :] = key_ref[0]
    forward_ref[ROWS : 2 * ROWS, :] = value_ref[0]
    forward_ref[2 * ROWS :, :] = wide_ids(ids_ref)


def split_kernel(query_ref, kept_ref, near_ref):
    t = lax.axis_index("tp").astype(jnp.int32)
    for apart in range(PIECES):
        lo = pl.multiple_of((t ^ apart) * 1024, 1024)
        ref = near_ref if apart & 1 else kept_ref
        ref[apart >> 1] = query_ref[:, pl.ds(lo, 1024)]


def pass_on_kernel(kept_ref, near_ref, forward_ref, forward_before_ref, far_ref, forward_pair_ref):
    far_ref[0] = kept_ref[1]
    far_ref[1] = near_ref[1]
    forward_pair_ref[0] = forward_before_ref[...]
    forward_pair_ref[1] = forward_ref[...]


def outgoing_kernel(cuts_ref, own_ref, outgoing_ref):
    f, y, upper = fsdp_place()
    side = jnp.where(lax.axis_index("section") < 4, 2 * PIECES, 0)
    row = jnp.where(upper, PIECES, 0)

    def whole(first):
        cuts = [cuts_ref[first + piece] for piece in range(PIECES)]
        ids = cuts[0][2 * PIECE :]
        return jnp.concatenate(
            [cut[:PIECE] for cut in cuts] + [cut[PIECE : 2 * PIECE] for cut in cuts] + [ids],
            axis=0,
        )

    own = whole(side + row)
    crossed = whole(side + PIECES - row)
    own_ref[...] = own
    for target in range(SPAN):
        outgoing_ref[target] = jnp.where(upper & (target <= y), crossed, own)


def reduce_kernel(parts_ref, own_part_ref, *refs):
    same_ref, other_ref = refs[-2:]
    f, y, upper = fsdp_place()
    same = own_part_ref[...]
    other = jnp.zeros((2 * ROWS, HEAD_DIM), jnp.float32)
    for source in range(SPAN):
        part = parts_ref[source].astype(jnp.float32)
        later = source > y
        same = same + jnp.where(later, part, 0.0)
        other = other + jnp.where(later, 0.0, part)
    same_ref[...] = same
    other_ref[...] = other.astype(jnp.bfloat16)


def finish_kernel(same_ref, from_upper_ref, from_nine_ref, key_grad_ref, value_grad_ref):
    f, y, upper = fsdp_place()
    late = from_upper_ref[...].astype(jnp.float32) + from_nine_ref[...].astype(jnp.float32)
    final = same_ref[...] + jnp.where(upper, 0.0, late)
    key_grad_ref[0] = (final[:ROWS] * (1.0 / math.sqrt(HEAD_DIM))).astype(jnp.bfloat16)
    value_grad_ref[0] = final[ROWS:].astype(jnp.bfloat16)


def run_small(kernel, name, limit, shapes, *arrays, waits=(), flops=0):
    return pl.pallas_call(
        kernel,
        out_shape=tuple(
            jax.ShapeDtypeStruct(shape[:-1] if shape[-1] is jnp.float32 else shape, jnp.float32)
            if shape[-1] is jnp.float32
            else jax.ShapeDtypeStruct(shape, jnp.bfloat16)
            for shape in shapes
        ),
        in_specs=[VMEM] * len(arrays) + [ANY] * len(waits),
        out_specs=(VMEM,) * len(shapes),
        compiler_params=pltpu.CompilerParams(vmem_limit_bytes=limit) if limit else None,
        cost_estimate=pl.CostEstimate(flops=int(flops), bytes_accessed=0, transcendentals=0)
        if flops
        else None,
        name=name,
    )(*arrays, *waits)


def run_forward(query, *pairs):
    return pl.pallas_call(
        forward_kernel,
        out_shape=(
            jax.ShapeDtypeStruct((ROWS, 1024), jnp.bfloat16),
            jax.ShapeDtypeStruct((8, 128), jnp.float32),
        ),
        in_specs=[VMEM] * 6,
        out_specs=(VMEM, VMEM),
        scratch_shapes=[
            pltpu.VMEM((KEYS, HEAD_DIM), jnp.bfloat16),
            pltpu.VMEM((HEAD_DIM, KEYS), jnp.bfloat16),
            pltpu.VMEM((KEYS, ROWS), jnp.float32),
            pltpu.VMEM((KEYS, 2 * ROWS), jnp.float32),
        ],
        compiler_params=pltpu.CompilerParams(vmem_limit_bytes=VMEM_LIMIT),
        cost_estimate=pl.CostEstimate(
            flops=2 * 2 * 1024 * KEYS * 128, bytes_accessed=3_000_000, transcendentals=1024 * KEYS
        ),
        name="forward_attention",
    )(query, *pairs)


def run_backward(queries, own, slots, nine, grad, *waits):
    return pl.pallas_call(
        backward_kernel,
        out_shape=(
            jax.ShapeDtypeStruct((ROWS, 1024), jnp.bfloat16),
            jax.ShapeDtypeStruct((SPAN, 2 * ROWS, HEAD_DIM), jnp.bfloat16),
            jax.ShapeDtypeStruct((2 * ROWS, HEAD_DIM), jnp.bfloat16),
            jax.ShapeDtypeStruct((2 * ROWS, HEAD_DIM), jnp.float32),
        ),
        in_specs=[VMEM] * 7 + [ANY] * len(waits),
        out_specs=(VMEM, VMEM, VMEM, VMEM),
        scratch_shapes=[
            pltpu.VMEM((ROWS, 1024), jnp.bfloat16),
            pltpu.VMEM((KEYS, HEAD_DIM), jnp.bfloat16),
            pltpu.VMEM((HEAD_DIM, KEYS), jnp.bfloat16),
            pltpu.VMEM((KEYS, HEAD_DIM), jnp.bfloat16),
            pltpu.VMEM((KEYS, ROWS), jnp.float32),
            pltpu.VMEM((KEYS, 2 * ROWS), jnp.float32),
            pltpu.VMEM((KEYS, 2 * ROWS), jnp.float32),
            pltpu.VMEM((KEYS, HEAD_DIM), jnp.float32),
            pltpu.VMEM((KEYS, HEAD_DIM), jnp.float32),
        ],
        compiler_params=pltpu.CompilerParams(vmem_limit_bytes=VMEM_LIMIT),
        cost_estimate=pl.CostEstimate(
            flops=1_000_000, bytes_accessed=0, transcendentals=0
        ),
        name="backward_attention",
    )(*queries, own, slots, nine, grad, *waits)


def local(
    queries,
    key_rows,
    values,
    segments,
    held_queries,
    held_keys,
    held_values,
    held_segments,
    out_grad,
):
    query_back = lax.ppermute(held_queries[0], "section", SECTION_PAIRS)
    cuts, forward_part = run_small(
        prepare_kernel,
        "prepare",
        None,
        ((4 * PIECES, CUT, 128), (BLOCK, 128)),
        held_keys,
        held_values,
        held_segments,
        key_rows,
        values,
        segments,
    )
    cuts = lax.all_to_all(
        cuts,
        ("section", "fsdp", "tp"),
        split_axis=0,
        concat_axis=0,
        tiled=False,
        axis_index_groups=MIRROR_GROUPS,
    )
    forward_before = lax.ppermute(forward_part, "fsdp", FSDP_UP[1])
    kept, near = run_small(
        split_kernel, "split", SMALL_LIMIT, ((2, PIECE, 1024),) * 2, query_back, flops=3e10
    )
    near = lax.ppermute(near, "tp", TP_NEAR)
    own, outgoing = run_small(
        outgoing_kernel,
        "outgoing",
        SMALL_LIMIT,
        ((BLOCK, 128), (SPAN, BLOCK, 128)),
        cuts,
    )
    slots = lax.all_to_all(
        outgoing, "fsdp", split_axis=0, concat_axis=0, tiled=False, axis_index_groups=ROW_GROUPS
    )
    far, forward_pair = run_small(
        pass_on_kernel,
        "pass_on",
        SMALL_LIMIT,
        ((2, PIECE, 1024), (2, BLOCK, 128)),
        kept,
        near,
        forward_part,
        forward_before,
        flops=3e10,
    )
    far = lax.ppermute(far, "tp", TP_FAR)
    nine = lax.ppermute(own, "fsdp", FSDP_NINE)
    pairs = {d: lax.ppermute(forward_pair, "fsdp", FSDP_UP[d]) for d in (8, 6, 4, 2)}

    query_grad, send, send_nine, own_part = run_backward(
        (kept, near, far), own, slots, nine, out_grad[0], pairs[4]
    )
    parts = lax.all_to_all(
        send, "fsdp", split_axis=0, concat_axis=0, tiled=False, axis_index_groups=ROW_GROUPS
    )
    from_nine = lax.ppermute(send_nine, "fsdp", FSDP_NINE)
    attn_out, mark = run_forward(queries[0], forward_pair, pairs[2], pairs[4], pairs[6], pairs[8])

    same_row, other_row = run_small(
        reduce_kernel,
        "reduce",
        SMALL_LIMIT,
        ((2 * ROWS, 128, jnp.float32), (2 * ROWS, 128)),
        parts,
        own_part,
        waits=(),
    )
    from_upper = lax.ppermute(other_row, "fsdp", FSDP_SWAP)
    key_grad, value_grad = run_small(
        finish_kernel,
        "finish",
        SMALL_LIMIT,
        ((1, ROWS, 128), (1, ROWS, 128)),
        same_row,
        from_upper,
        from_nine,
    )
    return (attn_out[None], query_grad[None], key_grad, value_grad)


def solution(mesh):
    return jax.shard_map(
        local,
        mesh=mesh,
        in_specs=(
            P("section", "fsdp", "tp"),
            P("section", "fsdp", "tp"),
            P("section", "fsdp", "tp"),
            P("section", "fsdp"),
            P("section", ("fsdp", "tp"), None),
            P("section", ("fsdp", "tp"), None),
            P("section", ("fsdp", "tp"), None),
            P("section", "fsdp"),
            P("section", "fsdp", "tp"),
        ),
        out_specs=(
            P("section", "fsdp", "tp"),
            P("section", "fsdp", "tp"),
            P("section", "fsdp", "tp"),
            P("section", "fsdp", "tp"),
        ),
        check_vma=False,
    )
```
